512 devices in a mesh: seq: 64 (over y, x, core), tp: 8 (over z).
Axes of the slice: x: 4, y: 8, z: 8, core: 2. Of those that a mesh axis runs over, the one named last changes fastest.
Arguments:
- q_nope: bfloat16 [4096, 128, 128], P('seq', 'tp'), may hold values from -6 to 6
- q_rope: bfloat16 [4096, 8192], P('seq', 'tp'), may hold values from -16 to 16
- index_queries: bfloat16 [4096, 8192], P('seq', 'tp'), may hold values from -6 to 6
- index_weights: bfloat16 [4096, 64], P('seq', 'tp'), may hold values from -6 to 6
- owner_offsets: int32 [4096, 2], P('seq'), may hold values from 0 to 62, all different within a row; in each aligned block of 64 rows (0 to 63, 64 to 127, ...) at most 4 rows name the same one
- local_blocks: int32 [4096, 2], P('seq'), may hold values from 0 to 13
- key_absorb_weight: bfloat16 [128, 128, 512], P('tp', 'seq'), may hold values from -0.5 to 0.5
- value_expand_weight: bfloat16 [128, 512, 128], P('tp', 'seq'), may hold values from -0.25 to 0.25
- cached_latents: bfloat16 [114688, 512], P('seq'), may hold values from -6 to 6
- rope_keys: bfloat16 [64, 114688], P(None, 'seq'), may hold values from -16 to 16
- index_keys: bfloat16 [114688, 128], P('seq'), may hold values from -6 to 6
Outputs:
- attended: bfloat16 [4096, 16384], P('seq', 'tp')
- index_scores: float32 [4096, 2048], P('seq', 'tp')
The draws below stay inside these ranges and needn't reach their ends.
Inputs may be any that keep to these rules, and one draw needn't show every extreme that they name: `owner_offsets`: each token names 2 different offsets; the 64 tokens of one index of seq name one offset at most 4 times, a bound that some block reaches.
All inputs are finite; a program needn't handle non-finite values.
Results may differ from the reference program's by a relative error of at most 0.01.
Values may be sent and summed in bfloat16 or wider, within the bound.
No kernel may reach another device: no remote copies, remote signals or barrier semaphores. Data moves between devices by JAX's collectives and lax.ppermute only.
A program may use at most 64 MiB of HBM per device.

```python
import math
import jax
import jax.numpy as jnp
import numpy as np
from jax import lax

ATTENTION_HEADS = 128
PLAIN_HEAD_SIZE = 128
ROPE = 64
LATENT_WIDTH = 512
VALUE_HEAD_SIZE = 128
IDX_HEADS = 64
IDX_DIM = 128
TOPK = 2048
BLOCK = 128
REMOTE_SEL = 2
TOK_DEV = 64
BLOCKS_PER_SHARD = 14
TOKENS = 4096
CONTEXT_LENGTH = 114688
SHARDS = 64
CAP = 4
N_SEQ = 64


def draw_q_rope(key, part):
    key = jax.random.fold_in(key, 7)
    noise_key = jax.random.fold_in(key, 0)
    base = jax.random.normal(noise_key, (TOKENS, ATTENTION_HEADS * ROPE), jnp.float32)
    return base.astype(jnp.bfloat16)


def draw_rope_keys(key, part):
    key = jax.random.fold_in(key, 11)
    base = jax.random.normal(key, (ROPE, CONTEXT_LENGTH), jnp.float32)
    return base.astype(jnp.bfloat16)


def touch_ends(entries, rng, low, high):
    spot = [jax.random.randint(jax.random.fold_in(rng, axis), (), 0, length) for axis, length in enumerate(entries.shape)]
    longest = entries.shape.index(max(entries.shape))
    beside = spot[:longest] + [(spot[longest] + 1) % entries.shape[longest]] + spot[longest + 1:]
    return entries.at[tuple(spot)].set(low).at[tuple(beside)].set(high)


def steps_of(own_key, shape, pieces, least, top_value):
    gain, own = 1.0, jax.random.fold_in(own_key, 6)
    for axis_at, parts in pieces:
        steps = jnp.exp(jax.random.uniform(jax.random.fold_in(own, axis_at), (parts,), jnp.float32, least / len(pieces), top_value / len(pieces)))
        gain = gain * jnp.repeat(steps, shape[axis_at] // parts).reshape([-1 if axis == axis_at else 1 for axis in range(len(shape))])
    return gain


def assign_block(own_key, own, number, rows, count, top, limit, slope):
    order = jax.random.permutation(own_key, count)
    packed, common = load_shares(count, rows * top, limit, slope, True), load_shares(count, rows * top, limit, slope, False)
    places = jnp.arange(count)

    def named(sizes, turn):
        used = int((sizes > 0).sum())
        fixed = max(1, used // 4)
        passed = fixed + (places - fixed + turn * (used - fixed)) % max(1, count - fixed)
        return jnp.zeros((count,), jnp.int32).at[order[jnp.where(places < fixed, places, passed)]].set(jnp.asarray(sizes, jnp.int32))

    sizes = jnp.where(number % 4 == 0, named(packed, number // 4), named(common, number - number // 4 - 1))
    mixed = jax.random.permutation(jax.random.fold_in(own, 3), count)
    source_of, sink = mixed[0:count // 2 * 2:2], mixed[1:count // 2 * 2:2]
    room = jnp.minimum(sizes[source_of] - 1, limit - sizes[sink]) // 2
    room = jnp.where((source_of == order[0]) | (sink == order[0]) | (sizes[sink] == 0), 0, jnp.maximum(room, 0))
    passed = jax.random.randint(jax.random.fold_in(own, 4), (count // 2,), 0, 1 << 20) % (room + 1)
    sizes = sizes.at[source_of].add(-passed).at[sink].add(passed)
    members = jnp.searchsorted(jnp.cumsum(sizes), jnp.arange(rows * top), side="right").astype(jnp.int32)
    grid = members.reshape(top, rows).T
    grid = grid[jax.random.permutation(jax.random.fold_in(own, 1), rows)]
    turn = jax.random.randint(jax.random.fold_in(own, 2), (rows, 1), 0, top)
    return jnp.take_along_axis(grid, (jnp.arange(top)[None, :] + turn) % top, axis=1)


def load_shares(amount, total, reach, slope, full):
    portions = [(1 << 20) // math.isqrt(rank ** slope) + 1 for rank in range(1, amount + 1)]
    largest = reach if full else min(reach, max(-(-total // amount), total * portions[0] // sum(portions)))
    least = 1 if total - largest >= amount - 1 else 0
    given, rest = [largest] + [least] * (amount - 1), total - largest - least * (amount - 1)
    while rest > 0:
        movable = [i for i in range(1, amount) if given[i] < largest] or [i for i in range(1, amount) if given[i] < reach]
        pool, left = sum([portions[i] for i in movable]), rest
        for i in movable:
            extra = min(reach - given[i], max(1, left * portions[i] // pool), rest)
            given[i] = given[i] + extra
            rest = rest - extra
    return np.array(given)


def gaussian(rng, extent, scale, most, cuts=(), kind=jnp.bfloat16):
    gain = steps_of(rng, extent, cuts, -0.22, 0.18) if cuts else 1.0
    drawn = jax.random.normal(rng, extent, jnp.float32) * scale * gain
    return jnp.minimum(jnp.maximum(drawn, -most), most).astype(kind)


def setup_inputs(seed: int = 0) -> dict:
    arg_keys = jax.random.split(jax.random.key(seed), 12)
    q_nope = gaussian(arg_keys[0], (TOKENS, ATTENTION_HEADS, PLAIN_HEAD_SIZE), 1.0, 6.0, ((0, 64), (1, 8)))
    q_rope = draw_q_rope(jax.random.fold_in(arg_keys[11], 71), 0)
    index_queries = gaussian(arg_keys[2], (TOKENS, IDX_HEADS * IDX_DIM), 1.0, 6.0, ((0, 64), (1, 8)))
    index_weights = gaussian(arg_keys[3], (TOKENS, IDX_HEADS), 1.0, 6.0, ((0, 64), (1, 8)))
    owner_offsets_keys = jax.random.split(jax.random.fold_in(arg_keys[4], 1), TOKENS // TOK_DEV)
    owner_offsets_turns = jax.random.permutation(jax.random.fold_in(arg_keys[4], 3), TOKENS // TOK_DEV)
    owner_offsets = jax.vmap(lambda own, number: assign_block(jax.random.fold_in(arg_keys[4], 2), own, number, TOK_DEV, SHARDS - 1, REMOTE_SEL, CAP, 2))(owner_offsets_keys, owner_offsets_turns).reshape((TOKENS, REMOTE_SEL))
    local_blocks = touch_ends(jax.random.randint(arg_keys[5], (TOKENS, REMOTE_SEL), 0, BLOCKS_PER_SHARD), jax.random.fold_in(arg_keys[5], 1), 0, BLOCKS_PER_SHARD - 1).astype(jnp.int32)
    key_absorb_weight = gaussian(arg_keys[6], (ATTENTION_HEADS, PLAIN_HEAD_SIZE, LATENT_WIDTH), PLAIN_HEAD_SIZE ** -0.5, 0.5, ((0, 8), (1, 64)))
    value_expand_weight = gaussian(arg_keys[7], (ATTENTION_HEADS, LATENT_WIDTH, VALUE_HEAD_SIZE), LATENT_WIDTH ** -0.5, 0.25, ((0, 8), (1, 64)))
    cached_latents = gaussian(arg_keys[8], (CONTEXT_LENGTH, LATENT_WIDTH), 1.0, 6.0, ((0, 64),))
    rope_keys = draw_rope_keys(jax.random.fold_in(arg_keys[11], 71), 0)
    index_keys = gaussian(arg_keys[10], (CONTEXT_LENGTH, IDX_DIM), 1.0, 6.0, ((0, 64),))
    return {"q_nope": q_nope, "q_rope": q_rope, "index_queries": index_queries, "index_weights": index_weights, "owner_offsets": owner_offsets, "local_blocks": local_blocks, "key_absorb_weight": key_absorb_weight, "value_expand_weight": value_expand_weight, "cached_latents": cached_latents, "rope_keys": rope_keys, "index_keys": index_keys}


def reference(q_nope, q_rope, index_queries, index_weights, owner_offsets, local_blocks, key_absorb_weight, value_expand_weight, cached_latents, rope_keys, index_keys):
    home = (jnp.arange(TOKENS, dtype=jnp.int32) // TOK_DEV).astype(jnp.int32)
    own_ids = home[:, None] * BLOCKS_PER_SHARD + jnp.arange(BLOCKS_PER_SHARD, dtype=jnp.int32)[None, :]
    owners = (home[:, None] + 1 + owner_offsets) % N_SEQ
    far_ids = owners * BLOCKS_PER_SHARD + local_blocks
    block_ids = jnp.concatenate([own_ids.astype(jnp.int32), far_ids.astype(jnp.int32)], axis=1).astype(jnp.int32)
    key_wide = key_absorb_weight.astype(jnp.float32)
    expanded_value = value_expand_weight.astype(jnp.float32)
    offsets = jnp.arange(BLOCK, dtype=jnp.int32)
    softmax_scale = 192.0 ** -0.5
    index_scale = (IDX_DIM * IDX_HEADS) ** -0.5

    def one_token(items):
        nope, rope_q, idx_q, idx_w, blocks = items
        q_latent = jnp.einsum("hd,hdc->hc", nope.astype(jnp.float32), key_wide).astype(jnp.bfloat16)
        positions = (blocks[:, None] * BLOCK + offsets[None, :]).astype(jnp.int32)
        latents = cached_latents[positions].astype(jnp.float32)
        rotary = rope_keys[:, positions].astype(jnp.float32)
        idx_keys = index_keys[positions].astype(jnp.float32)
        score = jnp.einsum("hc,kjc->hkj", q_latent.astype(jnp.float32), latents)
        score = score + jnp.einsum("hr,rkj->hkj", rope_q.reshape(ATTENTION_HEADS, ROPE).astype(jnp.float32), rotary)
        score = score * softmax_scale
        block_max = jnp.max(score, axis=2)
        expo = jnp.exp(score - block_max[:, :, None])
        block_total = jnp.sum(expo, axis=2)
        probs = expo.astype(jnp.bfloat16)
        latent_of_block = jnp.einsum("hkj,kjc->hkc", probs.astype(jnp.float32), latents).astype(jnp.bfloat16)
        near_max = block_max[:, :BLOCKS_PER_SHARD]
        local_max = jnp.max(near_max, axis=1)
        near_factor = jnp.exp(near_max - local_max[:, None])
        local_total = jnp.sum(block_total[:, :BLOCKS_PER_SHARD] * near_factor, axis=1)
        local_latent = (jnp.sum(latent_of_block[:, :BLOCKS_PER_SHARD].astype(jnp.float32) * near_factor[:, :, None], axis=1) / local_total[:, None]).astype(jnp.bfloat16)
        local_value = jnp.einsum("hc,hcv->hv", local_latent.astype(jnp.float32), expanded_value).astype(jnp.bfloat16)
        remote_value = jnp.einsum("nut,ntm->num", latent_of_block[:, BLOCKS_PER_SHARD:].astype(jnp.float32), expanded_value).astype(jnp.bfloat16)
        far_max = block_max[:, BLOCKS_PER_SHARD:]
        top = jnp.maximum(local_max, jnp.max(far_max, axis=1))
        near = jnp.exp(local_max - top) * local_total
        far = jnp.exp(far_max - top[:, None]) * block_total[:, BLOCKS_PER_SHARD:]
        summed = near[:, None] * local_value.astype(jnp.float32) + jnp.sum(far[:, :, None] * remote_value.astype(jnp.float32), axis=1)
        attended = summed / (near + jnp.sum(far, axis=1))[:, None]
        dots = jnp.einsum("gd,kjd->gkj", idx_q.reshape(IDX_HEADS, IDX_DIM).astype(jnp.float32), idx_keys)
        scores = jnp.einsum("g,gkj->kj", idx_w.astype(jnp.float32), jnp.maximum(dots, 0.0)) * index_scale
        return attended.astype(jnp.bfloat16).reshape(ATTENTION_HEADS * VALUE_HEAD_SIZE), scores.reshape(TOPK)

    attended, index_scores = lax.map(one_token, (q_nope, q_rope, index_queries, index_weights, block_ids))
    return attended, index_scores
```

```python
import jax
import jax.numpy as jnp
from jax import lax
from jax.experimental import pallas as pl
from jax.experimental.pallas import tpu as pltpu
from jax.sharding import Mesh
from jax.sharding import PartitionSpec as P

YS, XS, CS = 8, 4, 2
SHARDS = YS * XS * CS
TOK = 64
PICKS = 2
CAP = 4
SLOTS = SHARDS * CAP
ROWS = 2 * SLOTS
HEADS = 16
DIM = 128
ROPE = 64
LATENT = 512
VALUE = 128
IDX_HEADS = 8
IDX_DIM = 128
BLOCK = 128
BLOCKS = 14
SEEN = BLOCKS * BLOCK
GROUP = 16
CHUNK = 128
PER_CHUNK = CHUNK // GROUP
SORTED = 512
SEND = HEADS * DIM + 128
BACK = HEADS * VALUE // 2 + 128
SOFT_SCALE = 192.0 ** (-0.5)
INDEX_SCALE = (128 * 64) ** (-0.5)
F32 = jnp.float32
BF16 = jnp.bfloat16
LIMIT = 56 * 1024 * 1024


def dot(a, b, ca=1, cb=0):
    return lax.dot_general(a, b, (((ca,), (cb,)), ((), ())), preferred_element_type=F32)


def iota(shape, axis):
    return lax.broadcasted_iota(jnp.int32, shape, axis)


def ones_where(mask):
    return jnp.where(mask, 1.0, 0.0).astype(BF16)


def slots_of(dest):
    lane = iota((TOK, SHARDS), 1)
    named = [dest[:, i : i + 1] == lane for i in range(PICKS)]
    both = ones_where(jnp.logical_or(named[0], named[1]))
    below = ones_where(iota((TOK, TOK), 1) < iota((TOK, TOK), 0))
    earlier = dot(below, both)
    return [
        jnp.sum(jnp.where(n, earlier, 0.0), axis=1, keepdims=True).astype(jnp.int32) for n in named
    ]


def pack_kernel(dest_ref, blocks_ref, nope_ref, rope_ref, idx_ref, weights_ref, out_ref):
    dest = dest_ref[...]
    slot = slots_of(dest)
    row = iota((TOK, ROWS), 1)
    left = [row == dest[:, i : i + 1] * 8 + slot[i] for i in range(PICKS)]
    right = [row == dest[:, i : i + 1] * 8 + 4 + slot[i] for i in range(PICKS)]
    left_all = ones_where(jnp.logical_or(left[0], left[1]))
    right_all = ones_where(jnp.logical_or(right[0], right[1]))
    left_each = jnp.concatenate([ones_where(n) for n in left], axis=0)
    queries = jnp.concatenate([rope_ref[...], idx_ref[...]], axis=1)
    nope = nope_ref[...]
    half = SEND - 128
    both = jnp.concatenate([left_all, right_all], axis=0)
    data = jnp.concatenate([nope, queries], axis=0)
    out_ref[:, :half] = dot(both, data, 0, 0).astype(BF16)
    lane = iota((TOK, 128), 1)
    spread = dot(
        weights_ref[...], ones_where(iota((IDX_HEADS, 128), 0) == iota((IDX_HEADS, 128), 1))
    )
    extra = []
    for i in range(PICKS):
        number = blocks_ref[:, i : i + 1].astype(F32)
        extra.append(
            jnp.where(lane == 8, number, jnp.where(lane == 9, 1.0, spread)).astype(BF16)
        )
    out_ref[:, half:] = dot(left_each, jnp.concatenate(extra, axis=0), 0, 0).astype(BF16)


def pick_rows(offset):
    slot = iota((SLOTS, ROWS), 0)
    return ones_where(iota((SLOTS, ROWS), 1) == (slot // CAP) * 8 + offset + slot % CAP)


def far_index_kernel(sent_ref, keys_ref, out_ref, wide_ref):
    half = SEND - 128
    queries = dot(pick_rows(4), sent_ref[:, HEADS * ROPE : half]).astype(BF16)
    extra = dot(pick_rows(0), sent_ref[:, half:])
    block = extra[:, 8:9].astype(jnp.int32)
    for g in range(IDX_HEADS):
        wide_ref[g] = jnp.broadcast_to(extra[:, g : g + 1], (SLOTS, 128))
    result = jnp.zeros((SLOTS, BLOCK), F32)
    for b in range(0, BLOCKS, 2):
        keys = keys_ref[b * BLOCK : (b + 2) * BLOCK, :]
        sums = [jnp.zeros((SLOTS, BLOCK), F32) for _ in range(2)]
        for g in range(IDX_HEADS):
            dots = dot(queries[:, g * IDX_DIM : (g + 1) * IDX_DIM], keys, 1, 1)
            dots = jnp.maximum(dots, 0.0)
            for e in range(2):
                sums[e] = sums[e] + wide_ref[g] * dots[:, e * BLOCK : (e + 1) * BLOCK]
        for e in range(2):
            result = jnp.where(block == b + e, sums[e], result)
    out_ref[...] = result * INDEX_SCALE


def weight_kernel(all_ref, key_ref, value_ref):
    to, at = iota((256, 256), 0), iota((256, 256), 1)
    part = to - 128
    quarter, seq, row = part // 32, (part % 32) // 2, part % 2
    source = jnp.where(to < 128, (to // 8) * 16 + to % 8, seq * 16 + 8 + quarter * 2 + row)
    order = ones_where(at == source)
    for n in range(4):
        for lanes in range(0, 2048, 512):
            sorted_rows = dot(order, all_ref[n * 256 : (n + 1) * 256, lanes : lanes + 512])
            sorted_rows = sorted_rows.astype(BF16)
            value_ref[n * 128 : (n + 1) * 128, lanes : lanes + 512] = sorted_rows[:128]
            for q in range(4):
                key_ref[
                    n * 32 : (n + 1) * 32, q * 2048 + lanes : q * 2048 + lanes + 512
                ] = sorted_rows[128 + q * 32 : 160 + q * 32]


def far_kernel(
    sent_ref, key_ref, value_ref, lat_ref, rot_ref, out_ref,
    where_ref, ql_ref, qr_ref, lat_out_ref, full_ref,
):
    half = SEND - 128
    extra = dot(pick_rows(0), sent_ref[:, half:])
    lane = iota((SLOTS, 128), 1)
    block = extra[:, 8:9].astype(jnp.int32)
    filled = extra[:, 9:10] > 0.5
    mine = jnp.logical_and(lane == block, filled)
    one = ones_where(mine)
    upto = ones_where(iota((SLOTS, SLOTS), 1) <= iota((SLOTS, SLOTS), 0))
    running = dot(upto, one)
    rank = jnp.sum(jnp.where(mine, running, 0.0), axis=1, keepdims=True) - 1.0
    counts = dot(jnp.ones((8, SLOTS), BF16), one)
    groups = jnp.floor((counts + (GROUP - 1.0)) * (1.0 / GROUP))
    before = ones_where(iota((128, 128), 0) < iota((128, 128), 1))
    first = dot(groups.astype(BF16), before)
    last = (first + groups)[0:1, :]
    start = first[0:1, :]
    position = jnp.sum(jnp.where(mine, start, 0.0), axis=1, keepdims=True) * GROUP + rank
    position = jnp.where(filled, position, -1.0).astype(jnp.int32)
    where_ref[...] = ones_where(position == iota((SLOTS, SORTED), 1))
    total = jnp.max(last).astype(jnp.int32)
    narrow = iota((1, 128), 1)

    slot = iota((ROWS, SLOTS), 1)
    base = (slot // CAP) * 8 + slot % CAP
    to_left = ones_where(iota((ROWS, SLOTS), 0) == base)
    to_right = ones_where(iota((ROWS, SLOTS), 0) == base + 4)

    out_ref[...] = jnp.zeros_like(out_ref)

    def chunk(n, _):
        offset = pl.multiple_of(n * CHUNK, CHUNK)
        here = where_ref[:, pl.ds(offset, CHUNK)]
        left = dot(to_left, here).astype(BF16)
        right = dot(to_right, here).astype(BF16)
        nope = dot(left, sent_ref[:, : HEADS * DIM], 0, 0).astype(BF16)
        rope = dot(right, sent_ref[:, : HEADS * ROPE], 0, 0).astype(BF16)
        for h in range(HEADS):
            ql_ref[h] = dot(
                nope[:, h * DIM : (h + 1) * DIM], key_ref[:, h * LATENT : (h + 1) * LATENT]
            ).astype(BF16)
            qr_ref[h] = rope[:, h * ROPE : (h + 1) * ROPE]
        for j in range(PER_CHUNK):
            number = (n * PER_CHUNK + j).astype(F32)
            done = jnp.logical_and(narrow < BLOCKS, last <= number)
            at = jnp.minimum(jnp.sum(jnp.where(done, 1.0, 0.0)).astype(jnp.int32), BLOCKS - 1)
            begin = pl.multiple_of(at * BLOCK, BLOCK)
            latents = lat_ref[pl.ds(begin, BLOCK), :]
            rotary = rot_ref[:, pl.ds(begin, BLOCK)]
            rows = slice(j * GROUP, (j + 1) * GROUP)
            q = ql_ref[:, rows, :].reshape(HEADS * GROUP, LATENT)
            r = qr_ref[:, rows, :].reshape(HEADS * GROUP, ROPE)
            score = (dot(q, latents, 1, 1) + dot(r, rotary)) * SOFT_SCALE
            top = jnp.max(score, axis=1, keepdims=True)
            expo = jnp.exp(score - top)
            total_of = jnp.sum(expo, axis=1, keepdims=True)
            result = dot(expo.astype(BF16), latents).astype(BF16)
            lat_out_ref[:, rows, :] = result.reshape(HEADS, GROUP, LATENT)
            at_lane = iota((GROUP, 128), 1)
            tops = jnp.zeros((GROUP, 128), F32)
            sums = jnp.zeros((GROUP, 128), F32)
            for h in range(HEADS):
                sel = jnp.logical_and(at_lane % HEADS == h, at_lane < 3 * HEADS)
                part = slice(h * GROUP, (h + 1) * GROUP)
                tops = jnp.where(sel, top[part], tops)
                sums = jnp.where(sel, total_of[part], sums)
            for value, place in ((tops, BACK - 128), (sums, 2 * BACK - 128)):
                hi = value.astype(BF16).astype(F32)
                mid = (value - hi).astype(BF16).astype(F32)
                low = value - hi - mid
                split = jnp.where(at_lane < HEADS, hi, jnp.where(at_lane < 2 * HEADS, mid, low))
                full_ref[rows, place : place + 128] = split.astype(BF16)
        for h in range(HEADS):
            value = dot(lat_out_ref[h], value_ref[:, h * VALUE : (h + 1) * VALUE])
            place = h * VALUE if h < HEADS // 2 else h * VALUE + 128
            full_ref[:, place : place + VALUE] = value.astype(BF16)
        back = dot(left, full_ref[:, :BACK]) + dot(right, full_ref[:, BACK:])
        out_ref[...] = (out_ref[...].astype(F32) + back).astype(BF16)
        return 0

    lax.fori_loop(0, (total + PER_CHUNK - 1) // PER_CHUNK, chunk, 0)


def index_kernel(dest_ref, back_ref, idx_ref, weights_ref, keys_ref, out_ref, wide_ref):
    stacked = jnp.concatenate(
        [idx_ref[:, g * IDX_DIM : (g + 1) * IDX_DIM] for g in range(IDX_HEADS)], axis=0
    )
    weights = weights_ref[...].astype(F32)
    for g in range(IDX_HEADS):
        wide_ref[g] = jnp.broadcast_to(weights[:, g : g + 1], (TOK, 256))
    for b in range(0, BLOCKS, 2):
        keys = keys_ref[b * BLOCK : (b + 2) * BLOCK, :]
        dots = jnp.maximum(dot(stacked, keys, 1, 1), 0.0)
        acc = wide_ref[0] * dots[:TOK]
        for g in range(1, IDX_HEADS):
            acc = acc + wide_ref[g] * dots[g * TOK : (g + 1) * TOK]
        out_ref[:, b * BLOCK : (b + 2) * BLOCK] = acc * INDEX_SCALE
    back = back_ref[...]
    hi = back.astype(BF16)
    mid = (back - hi.astype(F32)).astype(BF16)
    low = (back - hi.astype(F32) - mid.astype(F32)).astype(BF16)
    dest = dest_ref[...]
    slot = slots_of(dest)
    lane = iota((TOK, SLOTS), 1)
    for i in range(PICKS):
        pick = ones_where(lane == dest[:, i : i + 1] * CAP + slot[i])
        far = dot(pick, hi) + dot(pick, mid) + dot(pick, low)
        out_ref[:, SEEN + i * BLOCK : SEEN + (i + 1) * BLOCK] = far


def near_kernel(nope_ref, rope_ref, key_ref, value_ref, lat_ref, rot_ref, out_ref, stat_ref):
    lane = iota((TOK, 128), 1)
    stat = jnp.zeros((TOK, 128), F32)
    step = 4
    for first in range(0, HEADS, step):
        heads = range(first, first + step)
        q = jnp.concatenate(
            [
                dot(
                    nope_ref[:, h * DIM : (h + 1) * DIM],
                    key_ref[:, h * LATENT : (h + 1) * LATENT],
                ).astype(BF16)
                for h in heads
            ],
            axis=0,
        )
        r = jnp.concatenate([rope_ref[:, h * ROPE : (h + 1) * ROPE] for h in heads], axis=0)
        score = (dot(q, lat_ref[...], 1, 1) + dot(r, rot_ref[...])) * SOFT_SCALE
        top = jnp.max(score, axis=1, keepdims=True)
        expo = jnp.exp(score - top)
        total = jnp.sum(expo, axis=1, keepdims=True)
        latent = (dot(expo.astype(BF16), lat_ref[...]) / total).astype(BF16)
        for n, h in enumerate(heads):
            part = slice(n * TOK, (n + 1) * TOK)
            value = dot(latent[part], value_ref[:, h * VALUE : (h + 1) * VALUE])
            out_ref[:, h * VALUE : (h + 1) * VALUE] = value.astype(BF16)
            stat = jnp.where(lane == h, top[part], stat)
            stat = jnp.where(lane == HEADS + h, total[part], stat)
    stat_ref[...] = stat


def combine_kernel(dest_ref, back_ref, near_ref, stat_ref, out_ref):
    dest = dest_ref[...]
    slot = slots_of(dest)
    row = iota((TOK, ROWS), 1)
    picks = [row == dest[:, i : i + 1] * 8 + o + slot[i] for i in range(PICKS) for o in (0, 4)]
    got = dot(jnp.concatenate([ones_where(p) for p in picks], axis=0), back_ref[...])
    far_top, far_sum = [], []
    for i in range(PICKS):
        tail = [got[(2 * i + e) * TOK : (2 * i + e + 1) * TOK, BACK - 128 :] for e in range(2)]
        whole = [
            t[:, :HEADS] + t[:, HEADS : 2 * HEADS] + t[:, 2 * HEADS : 3 * HEADS] for t in tail
        ]
        far_top.append(whole[0])
        far_sum.append(whole[1])
    near_top = stat_ref[:, :HEADS]
    near_sum = stat_ref[:, HEADS : 2 * HEADS]
    top = jnp.maximum(near_top, jnp.maximum(far_top[0], far_top[1]))
    near = jnp.exp(near_top - top) * near_sum
    far = [jnp.exp(far_top[i] - top) * far_sum[i] for i in range(PICKS)]
    whole = near + far[0] + far[1]
    near = near / whole
    far = [f / whole for f in far]
    for h in range(HEADS):
        e, place = (0, h) if h < HEADS // 2 else (1, h - HEADS // 2)
        lanes = slice(place * VALUE, (place + 1) * VALUE)
        value = near[:, h : h + 1] * near_ref[:, h * VALUE : (h + 1) * VALUE].astype(F32)
        for i in range(PICKS):
            part = got[(2 * i + e) * TOK : (2 * i + e + 1) * TOK, lanes]
            value = value + far[i][:, h : h + 1] * part
        out_ref[:, h * VALUE : (h + 1) * VALUE] = value.astype(BF16)


def call(kernel, out, scratch=(), name=None, flops=10**9, moved=10**6):
    return pl.pallas_call(
        kernel,
        out_shape=out,
        scratch_shapes=list(scratch),
        compiler_params=pltpu.CompilerParams(vmem_limit_bytes=LIMIT),
        cost_estimate=pl.CostEstimate(flops=flops, bytes_accessed=moved, transcendentals=0),
        name=name,
    )


def shape(dims, dtype=BF16):
    return jax.ShapeDtypeStruct(dims, dtype)


def pack(dest, blocks, nope, rope, idx, weights):
    return call(pack_kernel, shape((ROWS, SEND)), name="pack")(
        dest, blocks, nope, rope, idx, weights
    )


def far_index(sent, keys):
    return call(
        far_index_kernel,
        shape((SLOTS, BLOCK), F32),
        [pltpu.VMEM((IDX_HEADS, SLOTS, 128), F32)],
        name="far_index",
        flops=4 * 10**9,
    )(sent, keys)


def order_weights(gathered):
    return call(
        weight_kernel,
        [shape((DIM, HEADS * LATENT)), shape((LATENT, HEADS * VALUE))],
        name="order_weights",
        flops=4 * 10**9,
    )(gathered)


def far_attention(sent, key, value, lat, rot):
    return call(
        far_kernel,
        shape((ROWS, BACK)),
        [
            pltpu.VMEM((SLOTS, SORTED), BF16),
            pltpu.VMEM((HEADS, CHUNK, LATENT), BF16),
            pltpu.VMEM((HEADS, CHUNK, ROPE), BF16),
            pltpu.VMEM((HEADS, CHUNK, LATENT), BF16),
            pltpu.VMEM((CHUNK, 2 * BACK), BF16),
        ],
        name="far_attention",
        flops=8 * 10**9,
    )(sent, key, value, lat, rot)


def index_terms(dest, back, idx, weights, keys):
    return call(
        index_kernel,
        shape((TOK, SEEN + PICKS * BLOCK), F32),
        [pltpu.VMEM((IDX_HEADS, TOK, 256), F32)],
        name="index_terms",
    )(dest, back, idx, weights, keys)


def near_attention(nope, rope, key, value, lat, rot):
    return call(
        near_kernel,
        [shape((TOK, HEADS * VALUE)), shape((TOK, 128), F32)],
        name="near_attention",
        flops=8 * 10**9,
    )(nope, rope, key, value, lat, rot)


def combine(dest, back, near, stat):
    return call(combine_kernel, shape((TOK, HEADS * VALUE)), name="combine")(
        dest, back, near, stat
    )


SEQ = ("y", "x", "core")


def exchange(value):
    return lax.all_to_all(value, SEQ, split_axis=0, concat_axis=0, tiled=True)


def on_device(
    q_nope,
    q_rope,
    index_queries,
    index_weights,
    owner_offsets,
    local_blocks,
    key_absorb_weight,
    value_expand_weight,
    cached_latents,
    rope_keys,
    index_keys,
):
    here = lax.axis_index(SEQ)
    key_rows = jnp.transpose(key_absorb_weight.reshape(4, 4, 2, LATENT), (0, 2, 1, 3))
    value_rows = jnp.transpose(value_expand_weight, (1, 0, 2))
    shard = jnp.concatenate(
        [value_rows.reshape(8, HEADS * VALUE), key_rows.reshape(8, 4 * LATENT)], axis=0
    )
    gathered = lax.all_gather(shard, SEQ, axis=0, tiled=True)
    dest = (here + 1 + owner_offsets) % SHARDS
    nope = q_nope.reshape(TOK, HEADS * DIM)
    packed = pack(dest, local_blocks, nope, q_rope, index_queries, index_weights)
    sent = exchange(packed.reshape(SHARDS, 8, SEND)).reshape(ROWS, SEND)
    far_scores = far_index(sent, index_keys)
    far_scores = exchange(far_scores.reshape(SHARDS, CAP, BLOCK)).reshape(SLOTS, BLOCK)
    key, value = order_weights(gathered)
    back = far_attention(sent, key, value, cached_latents, rope_keys)
    back = exchange(back.reshape(SHARDS, 8, BACK)).reshape(ROWS, BACK)
    terms = index_terms(dest, far_scores, index_queries, index_weights, index_keys)
    index_scores = lax.psum_scatter(terms, "tp", scatter_dimension=1, tiled=True)
    near, stat = near_attention(nope, q_rope, key, value, cached_latents, rope_keys)
    attended = combine(dest, back, near, stat)
    return (attended, index_scores)


def solution(mesh):
    split = Mesh(mesh.devices.reshape(YS, XS, CS, mesh.shape["tp"]), ("y", "x", "core", "tp"))
    return jax.shard_map(
        on_device,
        mesh=split,
        in_specs=(
            P(SEQ, "tp", None),
            P(SEQ, "tp"),
            P(SEQ, "tp"),
            P(SEQ, "tp"),
            P(SEQ, None),
            P(SEQ, None),
            P("tp", SEQ, None),
            P("tp", SEQ, None),
            P(SEQ, None),
            P(None, SEQ),
            P(SEQ, None),
        ),
        out_specs=(P(SEQ, "tp"), P(SEQ, "tp")),
        check_vma=False,
    )
```

```python
import jax
import jax.numpy as jnp
from jax import lax
from jax.experimental import pallas as pl
from jax.experimental.pallas import tpu as pltpu
from jax.sharding import Mesh
from jax.sharding import PartitionSpec as P

YS, XS, CS = 8, 4, 2
SHARDS = YS * XS * CS
TOK = 64
PICKS = 2
CAP = 4
SLOTS = SHARDS * CAP
ROWS = 2 * SLOTS
HEADS = 16
DIM = 128
ROPE = 64
LATENT = 512
VALUE = 128
IDX_HEADS = 8
IDX_DIM = 128
BLOCK = 128
BLOCKS = 14
SEEN = BLOCKS * BLOCK
GROUP = 16
CHUNK = 128
PER_CHUNK = CHUNK // GROUP
SORTED = 512
SEND = HEADS * DIM + 128
BACK = HEADS * VALUE // 2 + 128
SOFT_SCALE = 192.0 ** (-0.5)
INDEX_SCALE = (128 * 64) ** (-0.5)
F32 = jnp.float32
BF16 = jnp.bfloat16


def dot(a, b, ca=1, cb=0):
    return lax.dot_general(a, b, (((ca,), (cb,)), ((), ())), preferred_element_type=F32)


def iota(shape, axis):
    return lax.broadcasted_iota(jnp.int32, shape, axis)


def ones_where(mask):
    return jnp.where(mask, 1.0, 0.0).astype(BF16)


def slots_of(dest):
    lane = iota((TOK, SHARDS), 1)
    named = [dest[:, i : i + 1] == lane for i in range(PICKS)]
    both = ones_where(jnp.logical_or(named[0], named[1]))
    below = ones_where(iota((TOK, TOK), 1) < iota((TOK, TOK), 0))
    earlier = dot(below, both)
    return [
        jnp.sum(jnp.where(n, earlier, 0.0), axis=1, keepdims=True).astype(jnp.int32) for n in named
    ]


def spread_out(value, rows):
    eye = ones_where(iota((rows, 128), 0) == iota((rows, 128), 1))
    return dot(value.astype(BF16), eye, 0, 0)


def pack_kernel(offsets_ref, blocks_ref, weights_ref, nope_ref, rope_ref, idx_ref, out_ref, place_ref):
    here = (lax.axis_index("y") * XS + lax.axis_index("x")) * CS + lax.axis_index("core")
    offsets = spread_out(offsets_ref[...].astype(F32), PICKS).astype(jnp.int32)
    numbers = spread_out(blocks_ref[...].astype(F32), PICKS)
    spread = spread_out(weights_ref[...], IDX_HEADS)
    dest = offsets + (here + 1)
    dest = jnp.where(dest >= SHARDS, dest - SHARDS, dest)
    slot = slots_of(dest)
    row = iota((TOK, ROWS), 1)
    at = [dest[:, i : i + 1] * 8 + slot[i] for i in range(PICKS)]
    left = [row == at[i] for i in range(PICKS)]
    right = [row == at[i] + 4 for i in range(PICKS)]
    lane = iota((TOK, 128), 1)
    place_ref[...] = jnp.where(lane == 0, at[0], at[1])
    left_all = ones_where(jnp.logical_or(left[0], left[1]))
    right_all = ones_where(jnp.logical_or(right[0], right[1]))
    left_each = jnp.concatenate([ones_where(n) for n in left], axis=0)
    queries = jnp.concatenate([rope_ref[...], idx_ref[...]], axis=1)
    half = SEND - 128
    both = jnp.concatenate([left_all, right_all], axis=0)
    data = jnp.concatenate([nope_ref[...], queries], axis=0)
    out_ref[:, :half] = dot(both, data, 0, 0).astype(BF16)
    extra = []
    for i in range(PICKS):
        number = numbers[:, i : i + 1]
        extra.append(
            jnp.where(lane == 8, number, jnp.where(lane == 9, 1.0, spread)).astype(BF16)
        )
    out_ref[:, half:] = dot(left_each, jnp.concatenate(extra, axis=0), 0, 0).astype(BF16)


def pick_rows(offset):
    slot = iota((SLOTS, ROWS), 0)
    return ones_where(iota((SLOTS, ROWS), 1) == (slot // CAP) * 8 + offset + slot % CAP)


def far_index_kernel(sent_ref, keys_ref, out_ref, where_ref, table_ref, wide_ref):
    half = SEND - 128
    queries = dot(pick_rows(4), sent_ref[:, HEADS * ROPE : half]).astype(BF16)
    extra = dot(pick_rows(0), sent_ref[:, half:])
    block = extra[:, 8:9].astype(jnp.int32)
    lane = iota((SLOTS, 128), 1)
    filled = extra[:, 9:10] > 0.5
    mine = jnp.logical_and(lane == block, filled)
    one = ones_where(mine)
    upto = ones_where(iota((SLOTS, SLOTS), 1) <= iota((SLOTS, SLOTS), 0))
    running = dot(upto, one)
    rank = jnp.sum(jnp.where(mine, running, 0.0), axis=1, keepdims=True) - 1.0

    def groups_of(counts):
        return jnp.floor((counts + (GROUP - 1.0)) * (1.0 / GROUP))

    row, column = iota((128, 128), 0), iota((128, 128), 1)
    groups = groups_of(dot(jnp.ones((8, SLOTS), BF16), one))
    first = dot(groups.astype(BF16), ones_where(row < column))[0:1, :]
    position = jnp.sum(jnp.where(mine, first, 0.0), axis=1, keepdims=True) * GROUP + rank
    position = jnp.where(filled, position, -1.0).astype(jnp.int32)
    where_ref[...] = ones_where(position == iota((SLOTS, SORTED), 1))
    down = groups_of(dot(one, jnp.ones((SLOTS, 128), BF16), 0, 0))
    last = dot(ones_where(column <= row), down.astype(BF16))
    done = jnp.logical_and(last <= column.astype(F32), row < BLOCKS)
    block_of = jnp.sum(jnp.where(done, 1.0, 0.0), axis=0, keepdims=True)
    block_of = jnp.minimum(block_of, BLOCKS - 1.0)
    total = jnp.max(last, axis=0, keepdims=True)
    table_ref[...] = jnp.where(iota((8, 128), 0) == 0, block_of, total).astype(jnp.int32)

    for g in range(IDX_HEADS):
        wide_ref[g] = jnp.broadcast_to(extra[:, g : g + 1], (SLOTS, 128))
    result = jnp.zeros((SLOTS, BLOCK), F32)
    for b in range(0, BLOCKS, 2):
        keys = keys_ref[b * BLOCK : (b + 2) * BLOCK, :]
        sums = [jnp.zeros((SLOTS, BLOCK), F32) for _ in range(2)]
        for g in range(IDX_HEADS):
            dots = dot(queries[:, g * IDX_DIM : (g + 1) * IDX_DIM], keys, 1, 1)
            dots = jnp.maximum(dots, 0.0)
            for e in range(2):
                sums[e] = sums[e] + wide_ref[g] * dots[:, e * BLOCK : (e + 1) * BLOCK]
        for e in range(2):
            result = jnp.where(block == b + e, sums[e], result)
    out_ref[...] = result * INDEX_SCALE


def order_weights(all_ref, key_ref, value_ref, ready=None):
    to, at = iota((256, 256), 0), iota((256, 256), 1)
    part = to - 128
    quarter, seq, row = part // 32, (part % 32) // 2, part % 2
    source = jnp.where(to < 128, (to // 8) * 16 + to % 8, seq * 16 + 8 + quarter * 2 + row)
    order = ones_where(at == source)
    for n in range(4):
        if ready is not None:
            ready[n].wait()
        for lanes in range(0, 2048, 512):
            sorted_rows = dot(order, all_ref[n * 256 : (n + 1) * 256, lanes : lanes + 512])
            sorted_rows = sorted_rows.astype(BF16)
            value_ref[n * 128 : (n + 1) * 128, lanes : lanes + 512] = sorted_rows[:128]
            for q in range(4):
                key_ref[
                    n * 32 : (n + 1) * 32, q * 2048 + lanes : q * 2048 + lanes + 512
                ] = sorted_rows[128 + q * 32 : 160 + q * 32]


def far_kernel(
    table_ref, sent_ref, where_ref, index_ref, rot_ref, all_ref, lat_ref, out_ref,
    buffer_ref, held_ref, key_ref, value_ref, ql_ref, qr_ref, lat_out_ref, full_ref, sems,
):
    parts = [
        pltpu.make_async_copy(
            all_ref.at[n * 256 : (n + 1) * 256], buffer_ref.at[n * 256 : (n + 1) * 256], sems.at[n]
        )
        for n in range(4)
    ]
    cache = pltpu.make_async_copy(lat_ref, held_ref, sems.at[4])
    for copy in parts:
        copy.start()
    cache.start()
    slot = iota((ROWS, SLOTS), 1)
    base = (slot // CAP) * 8 + slot % CAP
    to_left = ones_where(iota((ROWS, SLOTS), 0) == base)
    to_right = ones_where(iota((ROWS, SLOTS), 0) == base + 4)
    out_ref[:, : BACK - 128] = jnp.zeros((ROWS, BACK - 128), BF16)
    out_ref[:, BACK - 128 :] = dot(to_right, index_ref[...].astype(BF16)).astype(BF16)
    full_ref[:, 2 * BACK - 128 :] = jnp.zeros((CHUNK, 128), BF16)
    order_weights(buffer_ref, key_ref, value_ref, parts)
    cache.wait()

    def chunk(n, _):
        offset = pl.multiple_of(n * CHUNK, CHUNK)
        here = where_ref[:, pl.ds(offset, CHUNK)]
        left = dot(to_left, here).astype(BF16)
        right = dot(to_right, here).astype(BF16)
        nope = dot(left, sent_ref[:, : HEADS * DIM], 0, 0).astype(BF16)
        rope = dot(right, sent_ref[:, : HEADS * ROPE], 0, 0).astype(BF16)
        for h in range(HEADS):
            ql_ref[h] = dot(
                nope[:, h * DIM : (h + 1) * DIM], key_ref[:, h * LATENT : (h + 1) * LATENT]
            ).astype(BF16)
            qr_ref[h] = rope[:, h * ROPE : (h + 1) * ROPE]
        at_lane = iota((GROUP, 128), 1)
        for j in range(PER_CHUNK):
            begin = pl.multiple_of(table_ref[0, n * PER_CHUNK + j] * BLOCK, BLOCK)
            latents = held_ref[pl.ds(begin, BLOCK), :]
            rotary = rot_ref[:, pl.ds(begin, BLOCK)]
            rows = slice(j * GROUP, (j + 1) * GROUP)
            q = ql_ref[:, rows, :].reshape(HEADS * GROUP, LATENT)
            r = qr_ref[:, rows, :].reshape(HEADS * GROUP, ROPE)
            score = (dot(q, latents, 1, 1) + dot(r, rotary)) * SOFT_SCALE
            top = jnp.max(score, axis=1, keepdims=True)
            expo = jnp.exp(score - top)
            total_of = jnp.sum(expo, axis=1, keepdims=True)
            result = dot(expo.astype(BF16), latents).astype(BF16)
            lat_out_ref[:, rows, :] = result.reshape(HEADS, GROUP, LATENT)
            stat = jnp.zeros((GROUP, 128), F32)
            for h in range(HEADS):
                part = slice(h * GROUP, (h + 1) * GROUP)
                both = jnp.where(at_lane < 3 * HEADS, top[part], total_of[part])
                stat = jnp.where(at_lane % HEADS == h, both, stat)
            hi = stat.astype(BF16).astype(F32)
            mid = (stat - hi).astype(BF16).astype(F32)
            low = stat - hi - mid
            third = (at_lane // HEADS) % 3
            split = jnp.where(third == 0, hi, jnp.where(third == 1, mid, low))
            full_ref[rows, BACK - 128 : BACK] = split.astype(BF16)
        for h in range(HEADS):
            value = dot(lat_out_ref[h], value_ref[:, h * VALUE : (h + 1) * VALUE])
            place = h * VALUE if h < HEADS // 2 else h * VALUE + 128
            full_ref[:, place : place + VALUE] = value.astype(BF16)
        data = jnp.concatenate([full_ref[:, :BACK], full_ref[:, BACK:]], axis=0)
        back = dot(jnp.concatenate([left, right], axis=1), data)
        out_ref[...] = (out_ref[...].astype(F32) + back).astype(BF16)
        return 0

    lax.fori_loop(0, (table_ref[1, 0] + PER_CHUNK - 1) // PER_CHUNK, chunk, 0)


def index_kernel(idx_ref, weights_ref, keys_ref, out_ref, wide_ref):
    stacked = jnp.concatenate(
        [idx_ref[:, g * IDX_DIM : (g + 1) * IDX_DIM] for g in range(IDX_HEADS)], axis=0
    )
    weights = spread_out(weights_ref[...], IDX_HEADS)
    for g in range(IDX_HEADS):
        wide_ref[g] = jnp.broadcast_to(weights[:, g : g + 1], (TOK, 256))
    for b in range(0, BLOCKS, 2):
        keys = keys_ref[b * BLOCK : (b + 2) * BLOCK, :]
        dots = jnp.maximum(dot(stacked, keys, 1, 1), 0.0)
        acc = wide_ref[0] * dots[:TOK]
        for g in range(1, IDX_HEADS):
            acc = acc + wide_ref[g] * dots[g * TOK : (g + 1) * TOK]
        out_ref[b // 2] = acc * INDEX_SCALE
    out_ref[BLOCKS // 2] = jnp.zeros((TOK, 256), F32)


def near_kernel(
    nope_ref, rope_ref, all_ref, lat_ref, rot_ref, out_ref, stat_ref, key_ref, value_ref
):
    order_weights(all_ref, key_ref, value_ref)
    lane = iota((TOK, 128), 1)
    stat = jnp.zeros((TOK, 128), F32)
    step = 4
    for first in range(0, HEADS, step):
        heads = range(first, first + step)
        q = jnp.concatenate(
            [
                dot(
                    nope_ref[:, h * DIM : (h + 1) * DIM],
                    key_ref[:, h * LATENT : (h + 1) * LATENT],
                ).astype(BF16)
                for h in heads
            ],
            axis=0,
        )
        r = jnp.concatenate([rope_ref[:, h * ROPE : (h + 1) * ROPE] for h in heads], axis=0)
        score = (dot(q, lat_ref[...], 1, 1) + dot(r, rot_ref[...])) * SOFT_SCALE
        top = jnp.max(score, axis=1, keepdims=True)
        expo = jnp.exp(score - top)
        total = jnp.sum(expo, axis=1, keepdims=True)
        latent = (dot(expo.astype(BF16), lat_ref[...]) / total).astype(BF16)
        for n, h in enumerate(heads):
            part = slice(n * TOK, (n + 1) * TOK)
            value = dot(latent[part], value_ref[:, h * VALUE : (h + 1) * VALUE])
            out_ref[:, h * VALUE : (h + 1) * VALUE] = value.astype(BF16)
            stat = jnp.where(lane == h, top[part], stat)
            stat = jnp.where(lane == HEADS + h, total[part], stat)
    stat_ref[...] = stat


def combine_kernel(place_ref, back_ref, near_ref, stat_ref, own_ref, out_ref, index_ref):
    row = iota((TOK, ROWS), 1)
    picks = [row == place_ref[:, i : i + 1] + o for i in range(PICKS) for o in (0, 4)]
    got = dot(jnp.concatenate([ones_where(p) for p in picks], axis=0), back_ref[...])
    far_top, far_sum = [], []
    for i in range(PICKS):
        tail = got[2 * i * TOK : (2 * i + 1) * TOK, BACK - 128 :]
        whole = [tail[:, n * HEADS : (n + 1) * HEADS] for n in range(6)]
        far_top.append(whole[0] + whole[1] + whole[2])
        far_sum.append(whole[3] + whole[4] + whole[5])
        terms = got[(2 * i + 1) * TOK : (2 * i + 2) * TOK, BACK - 128 :]
        lanes = slice(i * BLOCK, (i + 1) * BLOCK)
        index_ref[:, lanes] = jnp.where(
            lax.axis_index("tp") == BLOCKS // 2, terms, own_ref[:, lanes]
        )
    near_top = stat_ref[:, :HEADS]
    near_sum = stat_ref[:, HEADS : 2 * HEADS]
    top = jnp.maximum(near_top, jnp.maximum(far_top[0], far_top[1]))
    near = jnp.exp(near_top - top) * near_sum
    far = [jnp.exp(far_top[i] - top) * far_sum[i] for i in range(PICKS)]
    whole = near + far[0] + far[1]
    near = near / whole
    far = [f / whole for f in far]
    for h in range(HEADS):
        e, place = (0, h) if h < HEADS // 2 else (1, h - HEADS // 2)
        lanes = slice(place * VALUE, (place + 1) * VALUE)
        value = near[:, h : h + 1] * near_ref[:, h * VALUE : (h + 1) * VALUE].astype(F32)
        for i in range(PICKS):
            part = got[(2 * i + e) * TOK : (2 * i + e + 1) * TOK, lanes]
            value = value + far[i][:, h : h + 1] * part
        out_ref[:, h * VALUE : (h + 1) * VALUE] = value.astype(BF16)


VMEM = pl.BlockSpec(memory_space=pltpu.VMEM)
SMEM = pl.BlockSpec(memory_space=pltpu.SMEM)


def call(kernel, out, scratch=(), name=None, flops=10**9, limit=16, **more):
    return pl.pallas_call(
        kernel,
        out_shape=out,
        scratch_shapes=list(scratch),
        compiler_params=pltpu.CompilerParams(vmem_limit_bytes=limit * 1024 * 1024),
        cost_estimate=pl.CostEstimate(flops=flops, bytes_accessed=10**6, transcendentals=0),
        name=name,
        **more,
    )


def shape(dims, dtype=BF16):
    return jax.ShapeDtypeStruct(dims, dtype)


def pack(offsets, blocks, weights, nope, rope, idx):
    out = [shape((ROWS, SEND)), shape((TOK, 128), jnp.int32)]
    return call(pack_kernel, out, name="pack")(offsets, blocks, weights, nope, rope, idx)


def far_index(sent, keys):
    out = [
        shape((SLOTS, BLOCK), F32),
        shape((SLOTS, SORTED)),
        shape((8, 128), jnp.int32),
    ]
    scratch = [pltpu.VMEM((IDX_HEADS, SLOTS, 128), F32)]
    return call(far_index_kernel, out, scratch, "far_index", 4 * 10**9)(sent, keys)


WEIGHTS = [
    pltpu.VMEM((DIM, HEADS * LATENT), BF16),
    pltpu.VMEM((LATENT, HEADS * VALUE), BF16),
]


def far_attention(table, sent, where, index, gathered, lat, rot):
    scratch = (
        [pltpu.VMEM((16 * SHARDS, 2048), BF16), pltpu.VMEM((SEEN, LATENT), BF16)]
        + WEIGHTS
        + [
            pltpu.VMEM((HEADS, CHUNK, LATENT), BF16),
            pltpu.VMEM((HEADS, CHUNK, ROPE), BF16),
            pltpu.VMEM((HEADS, CHUNK, LATENT), BF16),
            pltpu.VMEM((CHUNK, 2 * BACK), BF16),
            pltpu.SemaphoreType.DMA((5,)),
        ]
    )
    anywhere = pl.BlockSpec(memory_space=pl.ANY)
    return call(
        far_kernel,
        shape((ROWS, BACK)),
        scratch,
        "far_attention",
        8 * 10**9,
        32,
        in_specs=[SMEM] + [VMEM] * 4 + [anywhere] * 2,
    )(table, sent, where, index, rot, gathered, lat)


def index_terms(idx, weights, keys):
    scratch = [pltpu.VMEM((IDX_HEADS, TOK, 256), F32)]
    return call(index_kernel, shape((8, TOK, 256), F32), scratch, "index_terms")(
        idx, weights, keys
    )


def near_attention(nope, rope, gathered, lat, rot):
    out = [shape((TOK, HEADS * VALUE)), shape((TOK, 128), F32)]
    return call(near_kernel, out, WEIGHTS, "near_attention", 8 * 10**9, 32)(
        nope, rope, gathered, lat, rot
    )


def combine(place, back, near, stat, own):
    out = [shape((TOK, HEADS * VALUE)), shape((TOK, 256), F32)]
    return call(combine_kernel, out, name="combine")(place, back, near, stat, own)


SEQ = ("y", "x", "core")


def exchange(value):
    return lax.all_to_all(value, SEQ, split_axis=0, concat_axis=0, tiled=True)


def on_device(
    q_nope,
    q_rope,
    index_queries,
    index_weights,
    owner_offsets,
    local_blocks,
    key_absorb_weight,
    value_expand_weight,
    cached_latents,
    rope_keys,
    index_keys,
):
    key_rows = jnp.transpose(key_absorb_weight.reshape(4, 4, 2, LATENT), (0, 2, 1, 3))
    value_rows = jnp.transpose(value_expand_weight, (1, 0, 2))
    shard = jnp.concatenate(
        [value_rows.reshape(8, HEADS * VALUE), key_rows.reshape(8, 4 * LATENT)], axis=0
    )
    gathered = lax.all_gather(shard, SEQ, axis=0, tiled=True)
    weights = index_weights.T
    nope = q_nope.reshape(TOK, HEADS * DIM)
    packed, place = pack(owner_offsets.T, local_blocks.T, weights, nope, q_rope, index_queries)
    sent = exchange(packed.reshape(SHARDS, 8, SEND)).reshape(ROWS, SEND)
    terms = index_terms(index_queries, weights, index_keys)
    own = lax.psum_scatter(terms, "tp", scatter_dimension=0, tiled=False)
    index, where, table = far_index(sent, index_keys)
    for bit in (1, 2, 4):
        index = index + lax.ppermute(index, "tp", [(n, n ^ bit) for n in range(8)])
    back = far_attention(table, sent, where, index, gathered, cached_latents, rope_keys)
    back = exchange(back.reshape(SHARDS, 8, BACK)).reshape(ROWS, BACK)
    near, stat = near_attention(nope, q_rope, gathered, cached_latents, rope_keys)
    return combine(place, back, near, stat, own)


def solution(mesh):
    split = Mesh(mesh.devices.reshape(YS, XS, CS, mesh.shape["tp"]), ("y", "x", "core", "tp"))
    return jax.shard_map(
        on_device,
        mesh=split,
        in_specs=(
            P(SEQ, "tp", None),
            P(SEQ, "tp"),
            P(SEQ, "tp"),
            P(SEQ, "tp"),
            P(SEQ, None),
            P(SEQ, None),
            P("tp", SEQ, None),
            P("tp", SEQ, None),
            P(SEQ, None),
            P(None, SEQ),
            P(SEQ, None),
        ),
        out_specs=(P(SEQ, "tp"), P(SEQ, "tp")),
        check_vma=False,
    )
```

```python
import jax
import jax.numpy as jnp
from jax import lax
from jax.experimental import pallas as pl
from jax.experimental.pallas import tpu as pltpu
from jax.sharding import Mesh
from jax.sharding import PartitionSpec as P

YS, XS, CS = 8, 4, 2
SHARDS = YS * XS * CS
TOK = 64
PICKS = 2
CAP = 4
SLOTS = SHARDS * CAP
ROWS = 2 * SLOTS
HEADS = 16
DIM = 128
ROPE = 64
LATENT = 512
VALUE = 128
IDX_HEADS = 8
IDX_DIM = 128
BLOCK = 128
BLOCKS = 14
SEEN = BLOCKS * BLOCK
GROUP = 16
CHUNK = 256
BATCH = 4
PER_CHUNK = CHUNK // GROUP
SORTED = 512
SEND = HEADS * DIM + 128
BACK = HEADS * VALUE // 2 + 128
SOFT_SCALE = 192.0 ** (-0.5)
INDEX_SCALE = (128 * 64) ** (-0.5)
F32 = jnp.float32
BF16 = jnp.bfloat16


def dot(a, b, ca=1, cb=0):
    return lax.dot_general(a, b, (((ca,), (cb,)), ((), ())), preferred_element_type=F32)


def iota(shape, axis):
    return lax.broadcasted_iota(jnp.int32, shape, axis)


def ones_where(mask):
    return jnp.where(mask, 1.0, 0.0).astype(BF16)


def slots_of(dest):
    lane = iota((TOK, SHARDS), 1)
    named = [dest[:, i : i + 1] == lane for i in range(PICKS)]
    both = ones_where(jnp.logical_or(named[0], named[1]))
    below = ones_where(iota((TOK, TOK), 1) < iota((TOK, TOK), 0))
    earlier = dot(below, both)
    return [
        jnp.sum(jnp.where(n, earlier, 0.0), axis=1, keepdims=True).astype(jnp.int32) for n in named
    ]


def spread_out(value, rows):
    eye = ones_where(iota((rows, 128), 0) == iota((rows, 128), 1))
    return dot(value.astype(BF16), eye, 0, 0)


def pack_kernel(offsets_ref, blocks_ref, weights_ref, nope_ref, rope_ref, idx_ref, out_ref, place_ref):
    here = (lax.axis_index("y") * XS + lax.axis_index("x")) * CS + lax.axis_index("core")
    offsets = spread_out(offsets_ref[...].astype(F32), PICKS).astype(jnp.int32)
    numbers = spread_out(blocks_ref[...].astype(F32), PICKS)
    spread = spread_out(weights_ref[...], IDX_HEADS)
    dest = offsets + (here + 1)
    dest = jnp.where(dest >= SHARDS, dest - SHARDS, dest)
    slot = slots_of(dest)
    row = iota((TOK, ROWS), 1)
    at = [dest[:, i : i + 1] * 8 + slot[i] for i in range(PICKS)]
    left = [row == at[i] for i in range(PICKS)]
    right = [row == at[i] + 4 for i in range(PICKS)]
    lane = iota((TOK, 128), 1)
    place_ref[...] = jnp.where(lane == 0, at[0], at[1])
    left_all = ones_where(jnp.logical_or(left[0], left[1]))
    right_all = ones_where(jnp.logical_or(right[0], right[1]))
    left_each = jnp.concatenate([ones_where(n) for n in left], axis=0)
    queries = jnp.concatenate([rope_ref[...], idx_ref[...]], axis=1)
    half = SEND - 128
    both = jnp.concatenate([left_all, right_all], axis=0)
    data = jnp.concatenate([nope_ref[...], queries], axis=0)
    out_ref[:, :half] = dot(both, data, 0, 0).astype(BF16)
    extra = []
    for i in range(PICKS):
        number = numbers[:, i : i + 1]
        extra.append(
            jnp.where(lane == 8, number, jnp.where(lane == 9, 1.0, spread)).astype(BF16)
        )
    out_ref[:, half:] = dot(left_each, jnp.concatenate(extra, axis=0), 0, 0).astype(BF16)


def pick_rows(offset):
    slot = iota((SLOTS, ROWS), 0)
    return ones_where(iota((SLOTS, ROWS), 1) == (slot // CAP) * 8 + offset + slot % CAP)


def far_index_kernel(sent_ref, keys_ref, out_ref, where_ref, table_ref, wide_ref):
    half = SEND - 128
    queries = dot(pick_rows(4), sent_ref[:, HEADS * ROPE : half]).astype(BF16)
    extra = dot(pick_rows(0), sent_ref[:, half:])
    block = extra[:, 8:9].astype(jnp.int32)
    lane = iota((SLOTS, 128), 1)
    filled = extra[:, 9:10] > 0.5
    mine = jnp.logical_and(lane == block, filled)
    one = ones_where(mine)
    upto = ones_where(iota((SLOTS, SLOTS), 1) <= iota((SLOTS, SLOTS), 0))
    running = dot(upto, one)
    rank = jnp.sum(jnp.where(mine, running, 0.0), axis=1, keepdims=True) - 1.0

    def groups_of(counts):
        return jnp.floor((counts + (GROUP - 1.0)) * (1.0 / GROUP))

    row, column = iota((128, 128), 0), iota((128, 128), 1)
    groups = groups_of(dot(jnp.ones((8, SLOTS), BF16), one))
    first = dot(groups.astype(BF16), ones_where(row < column))[0:1, :]
    position = jnp.sum(jnp.where(mine, first, 0.0), axis=1, keepdims=True) * GROUP + rank
    position = jnp.where(filled, position, -1.0).astype(jnp.int32)
    where_ref[...] = ones_where(position == iota((SLOTS, SORTED), 1))
    down = groups_of(dot(one, jnp.ones((SLOTS, 128), BF16), 0, 0))
    last = dot(ones_where(column <= row), down.astype(BF16))
    done = jnp.logical_and(last <= column.astype(F32), row < BLOCKS)
    block_of = jnp.sum(jnp.where(done, 1.0, 0.0), axis=0, keepdims=True)
    block_of = jnp.minimum(block_of, BLOCKS - 1.0)
    total = jnp.max(last, axis=0, keepdims=True)
    table_ref[...] = jnp.where(iota((8, 128), 0) == 0, block_of, total).astype(jnp.int32)

    for g in range(IDX_HEADS):
        wide_ref[g] = jnp.broadcast_to(extra[:, g : g + 1], (SLOTS, 128))
    result = jnp.zeros((SLOTS, BLOCK), F32)
    for b in range(0, BLOCKS, 2):
        keys = keys_ref[b * BLOCK : (b + 2) * BLOCK, :]
        sums = [jnp.zeros((SLOTS, BLOCK), F32) for _ in range(2)]
        for g in range(IDX_HEADS):
            dots = dot(queries[:, g * IDX_DIM : (g + 1) * IDX_DIM], keys, 1, 1)
            dots = jnp.maximum(dots, 0.0)
            for e in range(2):
                sums[e] = sums[e] + wide_ref[g] * dots[:, e * BLOCK : (e + 1) * BLOCK]
        for e in range(2):
            result = jnp.where(block == b + e, sums[e], result)
    out_ref[...] = result * INDEX_SCALE


def order_weights(all_ref, key_ref, value_ref, ready=None):
    to, at = iota((256, 256), 0), iota((256, 256), 1)
    part = to - 128
    quarter, seq, row = part // 32, (part % 32) // 2, part % 2
    source = jnp.where(to < 128, (to // 8) * 16 + to % 8, seq * 16 + 8 + quarter * 2 + row)
    order = ones_where(at == source)
    for n in range(4):
        if ready is not None:
            ready[n].wait()
        for lanes in range(0, 2048, 512):
            sorted_rows = dot(order, all_ref[n * 256 : (n + 1) * 256, lanes : lanes + 512])
            sorted_rows = sorted_rows.astype(BF16)
            value_ref[n * 128 : (n + 1) * 128, lanes : lanes + 512] = sorted_rows[:128]
            for q in range(4):
                key_ref[
                    n * 32 : (n + 1) * 32, q * 2048 + lanes : q * 2048 + lanes + 512
                ] = sorted_rows[128 + q * 32 : 160 + q * 32]


def far_kernel(
    table_ref, sent_ref, where_ref, rot_ref, all_ref, lat_ref, out_ref,
    buffer_ref, held_ref, key_ref, value_ref, ql_ref, qr_ref, lat_out_ref, full_ref, sems,
):
    parts = [
        pltpu.make_async_copy(
            all_ref.at[n * 256 : (n + 1) * 256], buffer_ref.at[n * 256 : (n + 1) * 256], sems.at[n]
        )
        for n in range(4)
    ]
    cache = pltpu.make_async_copy(lat_ref, held_ref, sems.at[4])
    for copy in parts:
        copy.start()
    cache.start()
    slot = iota((ROWS, SLOTS), 1)
    base = (slot // CAP) * 8 + slot % CAP
    to_left = ones_where(iota((ROWS, SLOTS), 0) == base)
    to_right = ones_where(iota((ROWS, SLOTS), 0) == base + 4)
    out_ref[...] = jnp.zeros_like(out_ref)
    full_ref[:, 2 * BACK - 128 :] = jnp.zeros((CHUNK, 128), BF16)
    order_weights(buffer_ref, key_ref, value_ref, parts)
    cache.wait()

    def chunk(n, _):
        offset = pl.multiple_of(n * CHUNK, CHUNK)
        here = where_ref[:, pl.ds(offset, CHUNK)]
        left = dot(to_left, here).astype(BF16)
        right = dot(to_right, here).astype(BF16)
        nope = dot(left, sent_ref[:, : HEADS * DIM], 0, 0).astype(BF16)
        rope = dot(right, sent_ref[:, : HEADS * ROPE], 0, 0).astype(BF16)
        for h in range(HEADS):
            ql_ref[h] = dot(
                nope[:, h * DIM : (h + 1) * DIM], key_ref[:, h * LATENT : (h + 1) * LATENT]
            ).astype(BF16)
            qr_ref[h] = rope[:, h * ROPE : (h + 1) * ROPE]
        at_lane = iota((GROUP, 128), 1)
        for first in range(0, PER_CHUNK, BATCH):
            members = range(first, first + BATCH)
            caches, scores = [], []
            for j in members:
                begin = pl.multiple_of(table_ref[0, n * PER_CHUNK + j] * BLOCK, BLOCK)
                latents = held_ref[pl.ds(begin, BLOCK), :]
                rotary = rot_ref[:, pl.ds(begin, BLOCK)]
                rows = slice(j * GROUP, (j + 1) * GROUP)
                q = ql_ref[:, rows, :].reshape(HEADS * GROUP, LATENT)
                r = qr_ref[:, rows, :].reshape(HEADS * GROUP, ROPE)
                caches.append(latents)
                scores.append((dot(q, latents, 1, 1) + dot(r, rotary)) * SOFT_SCALE)
            tops = [jnp.max(score, axis=1, keepdims=True) for score in scores]
            expos = [jnp.exp(score - top) for score, top in zip(scores, tops)]
            totals = [jnp.sum(expo, axis=1, keepdims=True) for expo in expos]
            for j, latents, expo in zip(members, caches, expos):
                result = dot(expo.astype(BF16), latents).astype(BF16)
                rows = slice(j * GROUP, (j + 1) * GROUP)
                lat_out_ref[:, rows, :] = result.reshape(HEADS, GROUP, LATENT)
            for j, top, total_of in zip(members, tops, totals):
                stat = jnp.zeros((GROUP, 128), F32)
                for h in range(HEADS):
                    part = slice(h * GROUP, (h + 1) * GROUP)
                    both = jnp.where(at_lane < 3 * HEADS, top[part], total_of[part])
                    stat = jnp.where(at_lane % HEADS == h, both, stat)
                hi = stat.astype(BF16).astype(F32)
                mid = (stat - hi).astype(BF16).astype(F32)
                low = stat - hi - mid
                third = (at_lane // HEADS) % 3
                split = jnp.where(third == 0, hi, jnp.where(third == 1, mid, low))
                full_ref[j * GROUP : (j + 1) * GROUP, BACK - 128 : BACK] = split.astype(BF16)
        for h in range(HEADS):
            value = dot(lat_out_ref[h], value_ref[:, h * VALUE : (h + 1) * VALUE])
            place = h * VALUE if h < HEADS // 2 else h * VALUE + 128
            full_ref[:, place : place + VALUE] = value.astype(BF16)
        data = jnp.concatenate([full_ref[:, :BACK], full_ref[:, BACK:]], axis=0)
        back = dot(jnp.concatenate([left, right], axis=1), data)
        out_ref[...] = (out_ref[...].astype(F32) + back).astype(BF16)
        return 0

    lax.fori_loop(0, (table_ref[1, 0] + PER_CHUNK - 1) // PER_CHUNK, chunk, 0)


def index_kernel(place_ref, back_ref, idx_ref, weights_ref, keys_ref, out_ref, wide_ref):
    back = back_ref[...]
    hi = back.astype(BF16)
    mid = (back - hi.astype(F32)).astype(BF16)
    low = (back - hi.astype(F32) - mid.astype(F32)).astype(BF16)
    lane = iota((TOK, SLOTS), 1)
    for i in range(PICKS):
        at = place_ref[:, i : i + 1]
        pick = ones_where(lane == (at // 8) * CAP + at % 8)
        far = dot(pick, hi) + dot(pick, mid) + dot(pick, low)
        out_ref[BLOCKS // 2, :, i * BLOCK : (i + 1) * BLOCK] = far
    stacked = jnp.concatenate(
        [idx_ref[:, g * IDX_DIM : (g + 1) * IDX_DIM] for g in range(IDX_HEADS)], axis=0
    )
    weights = spread_out(weights_ref[...], IDX_HEADS)
    for g in range(IDX_HEADS):
        wide_ref[g] = jnp.broadcast_to(weights[:, g : g + 1], (TOK, 256))
    for b in range(0, BLOCKS, 2):
        keys = keys_ref[b * BLOCK : (b + 2) * BLOCK, :]
        dots = jnp.maximum(dot(stacked, keys, 1, 1), 0.0)
        acc = wide_ref[0] * dots[:TOK]
        for g in range(1, IDX_HEADS):
            acc = acc + wide_ref[g] * dots[g * TOK : (g + 1) * TOK]
        out_ref[b // 2] = acc * INDEX_SCALE


def near_kernel(
    nope_ref, rope_ref, all_ref, lat_ref, rot_ref, out_ref, stat_ref, key_ref, value_ref
):
    order_weights(all_ref, key_ref, value_ref)
    lane = iota((TOK, 128), 1)
    stat = jnp.zeros((TOK, 128), F32)
    step = 4
    for first in range(0, HEADS, step):
        heads = range(first, first + step)
        q = jnp.concatenate(
            [
                dot(
                    nope_ref[:, h * DIM : (h + 1) * DIM],
                    key_ref[:, h * LATENT : (h + 1) * LATENT],
                ).astype(BF16)
                for h in heads
            ],
            axis=0,
        )
        r = jnp.concatenate([rope_ref[:, h * ROPE : (h + 1) * ROPE] for h in heads], axis=0)
        score = (dot(q, lat_ref[...], 1, 1) + dot(r, rot_ref[...])) * SOFT_SCALE
        top = jnp.max(score, axis=1, keepdims=True)
        expo = jnp.exp(score - top)
        total = jnp.sum(expo, axis=1, keepdims=True)
        latent = (dot(expo.astype(BF16), lat_ref[...]) / total).astype(BF16)
        for n, h in enumerate(heads):
            part = slice(n * TOK, (n + 1) * TOK)
            value = dot(latent[part], value_ref[:, h * VALUE : (h + 1) * VALUE])
            out_ref[:, h * VALUE : (h + 1) * VALUE] = value.astype(BF16)
            stat = jnp.where(lane == h, top[part], stat)
            stat = jnp.where(lane == HEADS + h, total[part], stat)
    stat_ref[...] = stat


def combine_kernel(place_ref, back_ref, near_ref, stat_ref, out_ref):
    row = iota((TOK, ROWS), 1)
    picks = [row == place_ref[:, i : i + 1] + o for i in range(PICKS) for o in (0, 4)]
    got = dot(jnp.concatenate([ones_where(p) for p in picks], axis=0), back_ref[...])
    far_top, far_sum = [], []
    for i in range(PICKS):
        tail = got[2 * i * TOK : (2 * i + 1) * TOK, BACK - 128 :]
        whole = [tail[:, n * HEADS : (n + 1) * HEADS] for n in range(6)]
        far_top.append(whole[0] + whole[1] + whole[2])
        far_sum.append(whole[3] + whole[4] + whole[5])
    near_top = stat_ref[:, :HEADS]
    near_sum = stat_ref[:, HEADS : 2 * HEADS]
    top = jnp.maximum(near_top, jnp.maximum(far_top[0], far_top[1]))
    near = jnp.exp(near_top - top) * near_sum
    far = [jnp.exp(far_top[i] - top) * far_sum[i] for i in range(PICKS)]
    whole = near + far[0] + far[1]
    near = near / whole
    far = [f / whole for f in far]
    for h in range(HEADS):
        e, place = (0, h) if h < HEADS // 2 else (1, h - HEADS // 2)
        lanes = slice(place * VALUE, (place + 1) * VALUE)
        value = near[:, h : h + 1] * near_ref[:, h * VALUE : (h + 1) * VALUE].astype(F32)
        for i in range(PICKS):
            part = got[(2 * i + e) * TOK : (2 * i + e + 1) * TOK, lanes]
            value = value + far[i][:, h : h + 1] * part
        out_ref[:, h * VALUE : (h + 1) * VALUE] = value.astype(BF16)


VMEM = pl.BlockSpec(memory_space=pltpu.VMEM)
SMEM = pl.BlockSpec(memory_space=pltpu.SMEM)


def call(kernel, out, scratch=(), name=None, flops=10**9, limit=16, **more):
    return pl.pallas_call(
        kernel,
        out_shape=out,
        scratch_shapes=list(scratch),
        compiler_params=pltpu.CompilerParams(vmem_limit_bytes=limit * 1024 * 1024),
        cost_estimate=pl.CostEstimate(flops=flops, bytes_accessed=10**6, transcendentals=0),
        name=name,
        **more,
    )


def shape(dims, dtype=BF16):
    return jax.ShapeDtypeStruct(dims, dtype)


def pack(offsets, blocks, weights, nope, rope, idx):
    out = [shape((ROWS, SEND)), shape((TOK, 128), jnp.int32)]
    return call(pack_kernel, out, name="pack", limit=58)(offsets, blocks, weights, nope, rope, idx)


def far_index(sent, keys):
    out = [
        shape((SLOTS, BLOCK), F32),
        shape((SLOTS, SORTED)),
        shape((8, 128), jnp.int32),
    ]
    scratch = [pltpu.VMEM((IDX_HEADS, SLOTS, 128), F32)]
    return call(far_index_kernel, out, scratch, "far_index", 4 * 10**9)(sent, keys)


WEIGHTS = [
    pltpu.VMEM((DIM, HEADS * LATENT), BF16),
    pltpu.VMEM((LATENT, HEADS * VALUE), BF16),
]


def far_attention(table, sent, where, gathered, lat, rot):
    scratch = (
        [pltpu.VMEM((16 * SHARDS, 2048), BF16), pltpu.VMEM((SEEN, LATENT), BF16)]
        + WEIGHTS
        + [
            pltpu.VMEM((HEADS, CHUNK, LATENT), BF16),
            pltpu.VMEM((HEADS, CHUNK, ROPE), BF16),
            pltpu.VMEM((HEADS, CHUNK, LATENT), BF16),
            pltpu.VMEM((CHUNK, 2 * BACK), BF16),
            pltpu.SemaphoreType.DMA((5,)),
        ]
    )
    anywhere = pl.BlockSpec(memory_space=pl.ANY)
    return call(
        far_kernel,
        shape((ROWS, BACK)),
        scratch,
        "far_attention",
        8 * 10**9,
        59,
        in_specs=[SMEM] + [VMEM] * 3 + [anywhere] * 2,
    )(table, sent, where, rot, gathered, lat)


def index_terms(place, back, idx, weights, keys):
    scratch = [pltpu.VMEM((IDX_HEADS, TOK, 256), F32)]
    return call(index_kernel, shape((8, TOK, 256), F32), scratch, "index_terms")(
        place, back, idx, weights, keys
    )


def near_attention(nope, rope, gathered, lat, rot):
    out = [shape((TOK, HEADS * VALUE)), shape((TOK, 128), F32)]
    return call(near_kernel, out, WEIGHTS, "near_attention", 8 * 10**9, 32)(
        nope, rope, gathered, lat, rot
    )


def combine(place, back, near, stat):
    return call(combine_kernel, shape((TOK, HEADS * VALUE)), name="combine")(
        place, back, near, stat
    )


SEQ = ("y", "x", "core")


def exchange(value):
    return lax.all_to_all(value, SEQ, split_axis=0, concat_axis=0, tiled=True)


def on_device(
    q_nope,
    q_rope,
    index_queries,
    index_weights,
    owner_offsets,
    local_blocks,
    key_absorb_weight,
    value_expand_weight,
    cached_latents,
    rope_keys,
    index_keys,
):
    key_rows = jnp.transpose(key_absorb_weight.reshape(4, 4, 2, LATENT), (0, 2, 1, 3))
    value_rows = jnp.transpose(value_expand_weight, (1, 0, 2))
    shard = jnp.concatenate(
        [value_rows.reshape(8, HEADS * VALUE), key_rows.reshape(8, 4 * LATENT)], axis=0
    )
    gathered = lax.all_gather(shard, SEQ, axis=0, tiled=True)
    weights = index_weights.T
    nope = q_nope.reshape(TOK, HEADS * DIM)
    packed, place = pack(owner_offsets.T, local_blocks.T, weights, nope, q_rope, index_queries)
    sent = exchange(packed.reshape(SHARDS, 8, SEND)).reshape(ROWS, SEND)
    index, where, table = far_index(sent, index_keys)
    index = exchange(index.reshape(SHARDS, CAP, BLOCK)).reshape(SLOTS, BLOCK)
    terms = index_terms(place, index, index_queries, weights, index_keys)
    table, terms = lax.optimization_barrier((table, terms))
    index_scores = lax.psum_scatter(terms, "tp", scatter_dimension=0, tiled=False)
    back = far_attention(table, sent, where, gathered, cached_latents, rope_keys)
    back = exchange(back.reshape(SHARDS, 8, BACK)).reshape(ROWS, BACK)
    near, stat = near_attention(nope, q_rope, gathered, cached_latents, rope_keys)
    near, index_scores = lax.optimization_barrier((near, index_scores))
    attended = combine(place, back, near, stat)
    return (attended, index_scores)


def solution(mesh):
    split = Mesh(mesh.devices.reshape(YS, XS, CS, mesh.shape["tp"]), ("y", "x", "core", "tp"))
    return jax.shard_map(
        on_device,
        mesh=split,
        in_specs=(
            P(SEQ, "tp", None),
            P(SEQ, "tp"),
            P(SEQ, "tp"),
            P(SEQ, "tp"),
            P(SEQ, None),
            P(SEQ, None),
            P("tp", SEQ, None),
            P("tp", SEQ, None),
            P(SEQ, None),
            P(None, SEQ),
            P(SEQ, None),
        ),
        out_specs=(P(SEQ, "tp"), P(SEQ, "tp")),
        check_vma=False,
    )
```

```python
import jax
import jax.numpy as jnp
from jax import lax
from jax.experimental import pallas as pl
from jax.experimental.pallas import tpu as pltpu
from jax.sharding import Mesh
from jax.sharding import PartitionSpec as P

YS, XS, CS = 8, 4, 2
SHARDS = YS * XS * CS
TOK = 64
PICKS = 2
CAP = 4
SLOTS = SHARDS * CAP
ROWS = 2 * SLOTS
HEADS = 16
DIM = 128
ROPE = 64
LATENT = 512
VALUE = 128
IDX_HEADS = 8
IDX_DIM = 128
BLOCK = 128
BLOCKS = 14
SEEN = BLOCKS * BLOCK
GROUP = 16
CHUNK = 256
BATCH = 4
PER_CHUNK = CHUNK // GROUP
SORTED = 512
SEND = HEADS * DIM + 128
BACK = HEADS * VALUE // 2 + 128
SOFT_SCALE = 192.0 ** (-0.5)
INDEX_SCALE = (128 * 64) ** (-0.5)
F32 = jnp.float32
BF16 = jnp.bfloat16


def dot(a, b, ca=1, cb=0):
    return lax.dot_general(a, b, (((ca,), (cb,)), ((), ())), preferred_element_type=F32)


def iota(shape, axis):
    return lax.broadcasted_iota(jnp.int32, shape, axis)


def ones_where(mask):
    return jnp.where(mask, 1.0, 0.0).astype(BF16)


def slots_of(dest):
    lane = iota((TOK, SHARDS), 1)
    named = [dest[:, i : i + 1] == lane for i in range(PICKS)]
    both = ones_where(jnp.logical_or(named[0], named[1]))
    below = ones_where(iota((TOK, TOK), 1) < iota((TOK, TOK), 0))
    earlier = dot(below, both)
    return [
        jnp.sum(jnp.where(n, earlier, 0.0), axis=1, keepdims=True).astype(jnp.int32) for n in named
    ]


def spread_out(value, rows):
    eye = ones_where(iota((rows, 128), 0) == iota((rows, 128), 1))
    return dot(value.astype(BF16), eye, 0, 0)


def pack_kernel(offsets_ref, blocks_ref, weights_ref, nope_ref, rope_ref, idx_ref, out_ref, place_ref):
    here = (lax.axis_index("y") * XS + lax.axis_index("x")) * CS + lax.axis_index("core")
    offsets = spread_out(offsets_ref[...].astype(F32), PICKS).astype(jnp.int32)
    numbers = spread_out(blocks_ref[...].astype(F32), PICKS)
    spread = spread_out(weights_ref[...], IDX_HEADS)
    dest = offsets + (here + 1)
    dest = jnp.where(dest >= SHARDS, dest - SHARDS, dest)
    slot = slots_of(dest)
    row = iota((TOK, ROWS), 1)
    at = [dest[:, i : i + 1] * 8 + slot[i] for i in range(PICKS)]
    left = [row == at[i] for i in range(PICKS)]
    right = [row == at[i] + 4 for i in range(PICKS)]
    lane = iota((TOK, 128), 1)
    place_ref[...] = jnp.where(lane == 0, at[0], at[1])
    left_all = ones_where(jnp.logical_or(left[0], left[1]))
    right_all = ones_where(jnp.logical_or(right[0], right[1]))
    left_each = jnp.concatenate([ones_where(n) for n in left], axis=0)
    queries = jnp.concatenate([rope_ref[...], idx_ref[...]], axis=1)
    half = SEND - 128
    both = jnp.concatenate([left_all, right_all], axis=0)
    data = jnp.concatenate([nope_ref[...], queries], axis=0)
    out_ref[:, :half] = dot(both, data, 0, 0).astype(BF16)
    extra = []
    for i in range(PICKS):
        number = numbers[:, i : i + 1]
        extra.append(
            jnp.where(lane == 8, number, jnp.where(lane == 9, 1.0, spread)).astype(BF16)
        )
    out_ref[:, half:] = dot(left_each, jnp.concatenate(extra, axis=0), 0, 0).astype(BF16)


def pick_rows(offset):
    slot = iota((SLOTS, ROWS), 0)
    return ones_where(iota((SLOTS, ROWS), 1) == (slot // CAP) * 8 + offset + slot % CAP)


def far_index_kernel(sent_ref, keys_ref, out_ref, where_ref, table_ref, wide_ref):
    half = SEND - 128
    queries = dot(pick_rows(4), sent_ref[:, HEADS * ROPE : half]).astype(BF16)
    extra = dot(pick_rows(0), sent_ref[:, half:])
    block = extra[:, 8:9].astype(jnp.int32)
    lane = iota((SLOTS, 128), 1)
    filled = extra[:, 9:10] > 0.5
    mine = jnp.logical_and(lane == block, filled)
    one = ones_where(mine)
    upto = ones_where(iota((SLOTS, SLOTS), 1) <= iota((SLOTS, SLOTS), 0))
    running = dot(upto, one)
    rank = jnp.sum(jnp.where(mine, running, 0.0), axis=1, keepdims=True) - 1.0

    def groups_of(counts):
        return jnp.floor((counts + (GROUP - 1.0)) * (1.0 / GROUP))

    row, column = iota((128, 128), 0), iota((128, 128), 1)
    groups = groups_of(dot(jnp.ones((8, SLOTS), BF16), one))
    first = dot(groups.astype(BF16), ones_where(row < column))[0:1, :]
    position = jnp.sum(jnp.where(mine, first, 0.0), axis=1, keepdims=True) * GROUP + rank
    position = jnp.where(filled, position, -1.0).astype(jnp.int32)
    where_ref[...] = ones_where(position == iota((SLOTS, SORTED), 1))
    down = groups_of(dot(one, jnp.ones((SLOTS, 128), BF16), 0, 0))
    last = dot(ones_where(column <= row), down.astype(BF16))
    done = jnp.logical_and(last <= column.astype(F32), row < BLOCKS)
    block_of = jnp.sum(jnp.where(done, 1.0, 0.0), axis=0, keepdims=True)
    block_of = jnp.minimum(block_of, BLOCKS - 1.0)
    total = jnp.max(last, axis=0, keepdims=True)
    table_ref[...] = jnp.where(iota((8, 128), 0) == 0, block_of, total).astype(jnp.int32)

    for g in range(IDX_HEADS):
        wide_ref[g] = jnp.broadcast_to(extra[:, g : g + 1], (SLOTS, 128))
    result = jnp.zeros((SLOTS, BLOCK), F32)
    for b in range(0, BLOCKS, 2):
        keys = keys_ref[b * BLOCK : (b + 2) * BLOCK, :]
        sums = [jnp.zeros((SLOTS, BLOCK), F32) for _ in range(2)]
        for g in range(IDX_HEADS):
            dots = dot(queries[:, g * IDX_DIM : (g + 1) * IDX_DIM], keys, 1, 1)
            dots = jnp.maximum(dots, 0.0)
            for e in range(2):
                sums[e] = sums[e] + wide_ref[g] * dots[:, e * BLOCK : (e + 1) * BLOCK]
        for e in range(2):
            result = jnp.where(block == b + e, sums[e], result)
    out_ref[...] = result * INDEX_SCALE


def order_weights(all_ref, key_ref, value_ref, ready=None):
    to, at = iota((256, 256), 0), iota((256, 256), 1)
    part = to - 128
    quarter, seq, row = part // 32, (part % 32) // 2, part % 2
    source = jnp.where(to < 128, (to // 8) * 16 + to % 8, seq * 16 + 8 + quarter * 2 + row)
    order = ones_where(at == source)
    for n in range(4):
        if ready is not None:
            ready[n].wait()
        for lanes in range(0, 2048, 512):
            sorted_rows = dot(order, all_ref[n * 256 : (n + 1) * 256, lanes : lanes + 512])
            sorted_rows = sorted_rows.astype(BF16)
            value_ref[n * 128 : (n + 1) * 128, lanes : lanes + 512] = sorted_rows[:128]
            for q in range(4):
                key_ref[
                    n * 32 : (n + 1) * 32, q * 2048 + lanes : q * 2048 + lanes + 512
                ] = sorted_rows[128 + q * 32 : 160 + q * 32]


def far_kernel(
    table_ref, sent_ref, where_ref, rot_ref, all_ref, lat_ref, out_ref,
    buffer_ref, held_ref, key_ref, value_ref, ql_ref, qr_ref, lat_out_ref, full_ref, sems,
):
    parts = [
        pltpu.make_async_copy(
            all_ref.at[n * 256 : (n + 1) * 256], buffer_ref.at[n * 256 : (n + 1) * 256], sems.at[n]
        )
        for n in range(4)
    ]
    cache = pltpu.make_async_copy(lat_ref, held_ref, sems.at[4])
    for copy in parts:
        copy.start()
    cache.start()
    slot = iota((ROWS, SLOTS), 1)
    base = (slot // CAP) * 8 + slot % CAP
    to_left = ones_where(iota((ROWS, SLOTS), 0) == base)
    to_right = ones_where(iota((ROWS, SLOTS), 0) == base + 4)
    out_ref[...] = jnp.zeros_like(out_ref)
    full_ref[:, 2 * BACK - 128 :] = jnp.zeros((CHUNK, 128), BF16)
    order_weights(buffer_ref, key_ref, value_ref, parts)
    cache.wait()

    def chunk(n, _):
        offset = pl.multiple_of(n * CHUNK, CHUNK)
        here = where_ref[:, pl.ds(offset, CHUNK)]
        left = dot(to_left, here).astype(BF16)
        right = dot(to_right, here).astype(BF16)
        nope = dot(left, sent_ref[:, : HEADS * DIM], 0, 0).astype(BF16)
        rope = dot(right, sent_ref[:, : HEADS * ROPE], 0, 0).astype(BF16)
        for h in range(HEADS):
            ql_ref[h] = dot(
                nope[:, h * DIM : (h + 1) * DIM], key_ref[:, h * LATENT : (h + 1) * LATENT]
            ).astype(BF16)
            qr_ref[h] = rope[:, h * ROPE : (h + 1) * ROPE]
        at_lane = iota((GROUP, 128), 1)
        for first in range(0, PER_CHUNK, BATCH):
            members = range(first, first + BATCH)
            caches, scores = [], []
            for j in members:
                begin = pl.multiple_of(table_ref[0, n * PER_CHUNK + j] * BLOCK, BLOCK)
                latents = held_ref[pl.ds(begin, BLOCK), :]
                rotary = rot_ref[:, pl.ds(begin, BLOCK)]
                rows = slice(j * GROUP, (j + 1) * GROUP)
                q = ql_ref[:, rows, :].reshape(HEADS * GROUP, LATENT)
                r = qr_ref[:, rows, :].reshape(HEADS * GROUP, ROPE)
                caches.append(latents)
                scores.append((dot(q, latents, 1, 1) + dot(r, rotary)) * SOFT_SCALE)
            tops = [jnp.max(score, axis=1, keepdims=True) for score in scores]
            expos = [jnp.exp(score - top) for score, top in zip(scores, tops)]
            totals = [jnp.sum(expo, axis=1, keepdims=True) for expo in expos]
            for j, latents, expo in zip(members, caches, expos):
                result = dot(expo.astype(BF16), latents).astype(BF16)
                rows = slice(j * GROUP, (j + 1) * GROUP)
                lat_out_ref[:, rows, :] = result.reshape(HEADS, GROUP, LATENT)
            for j, top, total_of in zip(members, tops, totals):
                stat = jnp.zeros((GROUP, 128), F32)
                for h in range(HEADS):
                    part = slice(h * GROUP, (h + 1) * GROUP)
                    both = jnp.where(at_lane < 3 * HEADS, top[part], total_of[part])
                    stat = jnp.where(at_lane % HEADS == h, both, stat)
                hi = stat.astype(BF16).astype(F32)
                mid = (stat - hi).astype(BF16).astype(F32)
                low = stat - hi - mid
                third = (at_lane // HEADS) % 3
                split = jnp.where(third == 0, hi, jnp.where(third == 1, mid, low))
                full_ref[j * GROUP : (j + 1) * GROUP, BACK - 128 : BACK] = split.astype(BF16)
        for h in range(HEADS):
            value = dot(lat_out_ref[h], value_ref[:, h * VALUE : (h + 1) * VALUE])
            place = h * VALUE if h < HEADS // 2 else h * VALUE + 128
            full_ref[:, place : place + VALUE] = value.astype(BF16)
        data = jnp.concatenate([full_ref[:, :BACK], full_ref[:, BACK:]], axis=0)
        back = dot(jnp.concatenate([left, right], axis=1), data)
        out_ref[...] = (out_ref[...].astype(F32) + back).astype(BF16)
        return 0

    lax.fori_loop(0, (table_ref[1, 0] + PER_CHUNK - 1) // PER_CHUNK, chunk, 0)


def index_kernel(place_ref, back_ref, idx_ref, weights_ref, keys_ref, out_ref, wide_ref):
    back = back_ref[...]
    hi = back.astype(BF16)
    mid = (back - hi.astype(F32)).astype(BF16)
    low = (back - hi.astype(F32) - mid.astype(F32)).astype(BF16)
    lane = iota((TOK, SLOTS), 1)
    for i in range(PICKS):
        at = place_ref[:, i : i + 1]
        pick = ones_where(lane == (at // 8) * CAP + at % 8)
        far = dot(pick, hi) + dot(pick, mid) + dot(pick, low)
        out_ref[BLOCKS // 2, :, i * BLOCK : (i + 1) * BLOCK] = far
    stacked = jnp.concatenate(
        [idx_ref[:, g * IDX_DIM : (g + 1) * IDX_DIM] for g in range(IDX_HEADS)], axis=0
    )
    weights = spread_out(weights_ref[...], IDX_HEADS)
    for g in range(IDX_HEADS):
        wide_ref[g] = jnp.broadcast_to(weights[:, g : g + 1], (TOK, 256))
    for b in range(0, BLOCKS, 2):
        keys = keys_ref[b * BLOCK : (b + 2) * BLOCK, :]
        dots = jnp.maximum(dot(stacked, keys, 1, 1), 0.0)
        acc = wide_ref[0] * dots[:TOK]
        for g in range(1, IDX_HEADS):
            acc = acc + wide_ref[g] * dots[g * TOK : (g + 1) * TOK]
        out_ref[b // 2] = acc * INDEX_SCALE


def near_kernel(
    nope_ref, rope_ref, all_ref, lat_ref, rot_ref, out_ref, stat_ref, key_ref, value_ref
):
    order_weights(all_ref, key_ref, value_ref)
    lane = iota((TOK, 128), 1)
    stat = jnp.zeros((TOK, 128), F32)
    step = 4
    for first in range(0, HEADS, step):
        heads = range(first, first + step)
        q = jnp.concatenate(
            [
                dot(
                    nope_ref[:, h * DIM : (h + 1) * DIM],
                    key_ref[:, h * LATENT : (h + 1) * LATENT],
                ).astype(BF16)
                for h in heads
            ],
            axis=0,
        )
        r = jnp.concatenate([rope_ref[:, h * ROPE : (h + 1) * ROPE] for h in heads], axis=0)
        score = (dot(q, lat_ref[...], 1, 1) + dot(r, rot_ref[...])) * SOFT_SCALE
        top = jnp.max(score, axis=1, keepdims=True)
        expo = jnp.exp(score - top)
        total = jnp.sum(expo, axis=1, keepdims=True)
        latent = (dot(expo.astype(BF16), lat_ref[...]) / total).astype(BF16)
        for n, h in enumerate(heads):
            part = slice(n * TOK, (n + 1) * TOK)
            value = dot(latent[part], value_ref[:, h * VALUE : (h + 1) * VALUE])
            out_ref[:, h * VALUE : (h + 1) * VALUE] = value.astype(BF16)
            stat = jnp.where(lane == h, top[part], stat)
            stat = jnp.where(lane == HEADS + h, total[part], stat)
    stat_ref[...] = stat


def combine_kernel(place_ref, back_ref, near_ref, stat_ref, out_ref):
    row = iota((TOK, ROWS), 1)
    picks = [row == place_ref[:, i : i + 1] + o for i in range(PICKS) for o in (0, 4)]
    got = dot(jnp.concatenate([ones_where(p) for p in picks], axis=0), back_ref[...])
    far_top, far_sum = [], []
    for i in range(PICKS):
        tail = got[2 * i * TOK : (2 * i + 1) * TOK, BACK - 128 :]
        whole = [tail[:, n * HEADS : (n + 1) * HEADS] for n in range(6)]
        far_top.append(whole[0] + whole[1] + whole[2])
        far_sum.append(whole[3] + whole[4] + whole[5])
    near_top = stat_ref[:, :HEADS]
    near_sum = stat_ref[:, HEADS : 2 * HEADS]
    top = jnp.maximum(near_top, jnp.maximum(far_top[0], far_top[1]))
    near = jnp.exp(near_top - top) * near_sum
    far = [jnp.exp(far_top[i] - top) * far_sum[i] for i in range(PICKS)]
    whole = near + far[0] + far[1]
    near = near / whole
    far = [f / whole for f in far]
    for h in range(HEADS):
        e, place = (0, h) if h < HEADS // 2 else (1, h - HEADS // 2)
        lanes = slice(place * VALUE, (place + 1) * VALUE)
        value = near[:, h : h + 1] * near_ref[:, h * VALUE : (h + 1) * VALUE].astype(F32)
        for i in range(PICKS):
            part = got[(2 * i + e) * TOK : (2 * i + e + 1) * TOK, lanes]
            value = value + far[i][:, h : h + 1] * part
        out_ref[:, h * VALUE : (h + 1) * VALUE] = value.astype(BF16)


VMEM = pl.BlockSpec(memory_space=pltpu.VMEM)
SMEM = pl.BlockSpec(memory_space=pltpu.SMEM)


def call(kernel, out, scratch=(), name=None, flops=10**9, limit=16, **more):
    return pl.pallas_call(
        kernel,
        out_shape=out,
        scratch_shapes=list(scratch),
        compiler_params=pltpu.CompilerParams(vmem_limit_bytes=limit * 1024 * 1024),
        cost_estimate=pl.CostEstimate(flops=flops, bytes_accessed=10**6, transcendentals=0),
        name=name,
        **more,
    )


def shape(dims, dtype=BF16):
    return jax.ShapeDtypeStruct(dims, dtype)


def pack(offsets, blocks, weights, nope, rope, idx):
    out = [shape((ROWS, SEND)), shape((TOK, 128), jnp.int32)]
    return call(pack_kernel, out, name="pack", limit=58)(offsets, blocks, weights, nope, rope, idx)


def far_index(sent, keys):
    out = [
        shape((SLOTS, BLOCK), F32),
        shape((SLOTS, SORTED)),
        shape((8, 128), jnp.int32),
    ]
    scratch = [pltpu.VMEM((IDX_HEADS, SLOTS, 128), F32)]
    return call(far_index_kernel, out, scratch, "far_index", 4 * 10**9)(sent, keys)


WEIGHTS = [
    pltpu.VMEM((DIM, HEADS * LATENT), BF16),
    pltpu.VMEM((LATENT, HEADS * VALUE), BF16),
]


def far_attention(table, sent, where, gathered, lat, rot):
    scratch = (
        [pltpu.VMEM((16 * SHARDS, 2048), BF16), pltpu.VMEM((SEEN, LATENT), BF16)]
        + WEIGHTS
        + [
            pltpu.VMEM((HEADS, CHUNK, LATENT), BF16),
            pltpu.VMEM((HEADS, CHUNK, ROPE), BF16),
            pltpu.VMEM((HEADS, CHUNK, LATENT), BF16),
            pltpu.VMEM((CHUNK, 2 * BACK), BF16),
            pltpu.SemaphoreType.DMA((5,)),
        ]
    )
    anywhere = pl.BlockSpec(memory_space=pl.ANY)
    return call(
        far_kernel,
        shape((ROWS, BACK)),
        scratch,
        "far_attention",
        8 * 10**9,
        59,
        in_specs=[SMEM] + [VMEM] * 3 + [anywhere] * 2,
    )(table, sent, where, rot, gathered, lat)


def index_terms(place, back, idx, weights, keys):
    scratch = [pltpu.VMEM((IDX_HEADS, TOK, 256), F32)]
    return call(index_kernel, shape((8, TOK, 256), F32), scratch, "index_terms")(
        place, back, idx, weights, keys
    )


def near_attention(nope, rope, gathered, lat, rot):
    out = [shape((TOK, HEADS * VALUE)), shape((TOK, 128), F32)]
    return call(near_kernel, out, WEIGHTS, "near_attention", 8 * 10**9, 32)(
        nope, rope, gathered, lat, rot
    )


def combine(place, back, near, stat):
    return call(combine_kernel, shape((TOK, HEADS * VALUE)), name="combine")(
        place, back, near, stat
    )


SEQ = ("y", "x", "core")


def exchange(value):
    return lax.all_to_all(value, SEQ, split_axis=0, concat_axis=0, tiled=True)


def halves(terms, bit):
    upper = (lax.axis_index("tp") // bit) % 2
    sent = lax.dynamic_slice_in_dim(terms, (1 - upper) * bit, bit, 0)
    kept = lax.dynamic_slice_in_dim(terms, upper * bit, bit, 0)
    return kept, lax.ppermute(sent, "tp", [(n, n ^ bit) for n in range(8)])


def on_device(
    q_nope,
    q_rope,
    index_queries,
    index_weights,
    owner_offsets,
    local_blocks,
    key_absorb_weight,
    value_expand_weight,
    cached_latents,
    rope_keys,
    index_keys,
):
    key_rows = jnp.transpose(key_absorb_weight.reshape(4, 4, 2, LATENT), (0, 2, 1, 3))
    value_rows = jnp.transpose(value_expand_weight, (1, 0, 2))
    shard = jnp.concatenate(
        [value_rows.reshape(8, HEADS * VALUE), key_rows.reshape(8, 4 * LATENT)], axis=0
    )
    gathered = lax.all_gather(shard, SEQ, axis=0, tiled=True)
    weights = index_weights.T
    nope = q_nope.reshape(TOK, HEADS * DIM)
    packed, place = pack(owner_offsets.T, local_blocks.T, weights, nope, q_rope, index_queries)
    sent = exchange(packed.reshape(SHARDS, 8, SEND)).reshape(ROWS, SEND)
    index, where, table = far_index(sent, index_keys)
    index = exchange(index.reshape(SHARDS, CAP, BLOCK)).reshape(SLOTS, BLOCK)
    terms = index_terms(place, index, index_queries, weights, index_keys)
    table, terms = lax.optimization_barrier((table, terms))
    kept, other = halves(terms, 4)
    back = far_attention(table, sent, where, gathered, cached_latents, rope_keys)
    back = exchange(back.reshape(SHARDS, 8, BACK)).reshape(ROWS, BACK)
    near, stat = near_attention(nope, q_rope, gathered, cached_latents, rope_keys)
    near, other = lax.optimization_barrier((near, other))
    for bit in (2, 1):
        kept, other = halves(kept + other, bit)
    index_scores = (kept + other)[0]
    attended = combine(place, back, near, stat)
    return (attended, index_scores)


def solution(mesh):
    split = Mesh(mesh.devices.reshape(YS, XS, CS, mesh.shape["tp"]), ("y", "x", "core", "tp"))
    return jax.shard_map(
        on_device,
        mesh=split,
        in_specs=(
            P(SEQ, "tp", None),
            P(SEQ, "tp"),
            P(SEQ, "tp"),
            P(SEQ, "tp"),
            P(SEQ, None),
            P(SEQ, None),
            P("tp", SEQ, None),
            P("tp", SEQ, None),
            P(SEQ, None),
            P(None, SEQ),
            P(SEQ, None),
        ),
        out_specs=(P(SEQ, "tp"), P(SEQ, "tp")),
        check_vma=False,
    )
```
